32 devices in a mesh: row: 4 (over y, x), col: 8 (over z, core).
Axes of the slice: x: 2, y: 2, z: 4, core: 2. Of those that a mesh axis runs over, the one named last changes fastest.
Arguments:
- factor: float32 [4096, 4096], P('row', 'col'), may hold values from -1 to 2, as said below
- adjoint: float32 [4096, 4096], P('row', 'col'), may hold values from -6 to 6
Outputs:
- panel_adjoint: float32 [4096, 512], P('row')
The draws below stay inside these ranges and needn't reach their ends.
Inputs may be any that keep to these rules, and one draw needn't show every extreme that they name: In global order, every diagonal block of factor is lower triangular with diagonal entries from 1 to 2.
All inputs are finite; a program needn't handle non-finite values.
Results may differ from the reference program's by a relative error of at most 0.0003.
Values sent between devices are 32-bit elements; how exact they have to be, the bound alone decides.
No kernel may reach another device: no remote copies, remote signals or barrier semaphores. Data moves between devices by JAX's collectives and lax.ppermute only.
A program may use at most 192 MiB of HBM per device.

```python
import math
import jax
import jax.numpy as jnp
from jax import lax

NB = 256
BC = 2
ROWS_GRID = 4
COLS_GRID = 8
MB = 16
BR = 4
N = 4096


def draw_factor(key, part):
    normal_key, unit_key = jax.random.split(key)
    row_ids = jnp.arange(N, dtype=jnp.int32)
    block_of = row_ids // NB
    offset = row_ids % NB
    global_row = (block_of % BR * ROWS_GRID + block_of // BR) * NB + offset
    global_col = (block_of % BC * COLS_GRID + block_of // BC) * NB + offset
    spread = jnp.clip(jax.random.normal(normal_key, (N, N), jnp.float32), -6.0, 6.0)
    spread = spread * (1.0 / math.sqrt(N))
    unit = jax.random.uniform(unit_key, (N, N), jnp.float32)
    row_grid = global_row[:, None]
    col_grid = global_col[None, :]
    same_block = row_grid // NB == col_grid // NB
    inside = jnp.where(row_grid == col_grid, 1.0 + unit, jnp.where(row_grid > col_grid, (2.0 * unit - 1.0) * (0.9 / NB), 0.0))
    return jnp.where(same_block, inside, spread)


def block_levels(key, dims, cuts, smallest, high):
    factor_of, own = 1.0, jax.random.fold_in(key, 6)
    for axis_at, shards_of in cuts:
        heights = jnp.exp(jax.random.uniform(jax.random.fold_in(own, axis_at), (shards_of,), jnp.float32, smallest / len(cuts), high / len(cuts)))
        factor_of = factor_of * jnp.repeat(heights, dims[axis_at] // shards_of).reshape([-1 if axis == axis_at else 1 for axis in range(len(dims))])
    return factor_of


def scatter_about(rng, dims, scale, limit, cuts=(), held_as=jnp.bfloat16):
    factor_of = block_levels(rng, dims, cuts, -0.22, 0.18) if cuts else 1.0
    values = jax.random.normal(rng, dims, jnp.float32) * scale * factor_of
    return jnp.minimum(jnp.maximum(values, -limit), limit).astype(held_as)


def setup_inputs(seed: int = 0) -> dict:
    seeds = jax.random.split(jax.random.key(seed), 3)
    return {
        "factor": draw_factor(jax.random.fold_in(seeds[2], 71), 0),
        "adjoint": scatter_about(seeds[1], (N, N), 1.0, 6.0, ((0, 4), (1, 8)), jnp.float32),
    }


HIGHEST_PRECISION = lax.Precision.HIGHEST


def matmul(left_side, right_side):
    return jnp.dot(left_side, right_side, precision=HIGHEST_PRECISION, preferred_element_type=jnp.float32)


def tmatmul(left_side, right_side):
    return lax.dot_general(left_side, right_side, (((0,), (0,)), ((), ())), precision=HIGHEST_PRECISION, preferred_element_type=jnp.float32)


def lower_half(matrix):
    dimension = matrix.shape[0]
    positions = jnp.arange(dimension, dtype=jnp.int32)
    weight = jnp.where(positions[:, None] > positions[None, :], 1.0, jnp.where(positions[:, None] == positions[None, :], 0.5, 0.0))
    return matrix * weight.astype(matrix.dtype)


def inverse_lower(factor_block):
    dimension = factor_block.shape[0]
    if dimension == 1:
        return 1.0 / factor_block
    half_size = dimension // 2
    upper_inv = inverse_lower(factor_block[:half_size, :half_size])
    lower_inv = inverse_lower(factor_block[half_size:, half_size:])
    corner = -matmul(lower_inv, matmul(factor_block[half_size:, :half_size], upper_inv))
    zero_part = jnp.zeros((half_size, dimension - half_size), factor_block.dtype)
    top_rows = jnp.concatenate([upper_inv, zero_part], 1)
    bottom_rows = jnp.concatenate([corner, lower_inv], 1)
    return jnp.concatenate([top_rows, bottom_rows], 0)


def diagonal_adjoint(factor_block, block_bar, inverse):
    inner_part = lower_half(tmatmul(factor_block, block_bar))
    symmetric = tmatmul(inverse, matmul(inner_part, inverse))
    return lower_half(symmetric + symmetric.T)


def reference(factor, adjoint):
    row_ids = jnp.arange(N, dtype=jnp.int32)
    block_of = row_ids // NB
    offset = row_ids % NB
    global_row = ((block_of % BR) * ROWS_GRID + block_of // BR) * NB + offset
    global_col = ((block_of % BC) * COLS_GRID + block_of // BC) * NB + offset
    back_row = ((block_of % ROWS_GRID) * BR + block_of // ROWS_GRID) * NB + offset
    back_col = ((block_of % COLS_GRID) * BC + block_of // COLS_GRID) * NB + offset
    first_panel = factor[:, 0:NB][back_row]
    second_panel = factor[:, BC * NB:BC * NB + NB][back_row]
    first_bar = adjoint[:, 0:NB][back_row]
    second_bar = adjoint[:, BC * NB:BC * NB + NB][back_row]
    trailing = (row_ids >= 2 * NB)[:, None]
    panels = jnp.where(trailing, jnp.concatenate([first_panel, second_panel], 1), 0.0)
    by_row = panels[global_row]
    by_col = panels[global_col]

    def one_block(col_total, block_index):
        row_start = (block_index * NB).astype(jnp.int32)
        adjoint_strip = lax.dynamic_slice_in_dim(adjoint, row_start, NB, 0)
        strip_rows = lax.dynamic_slice_in_dim(global_row, row_start, NB, 0)
        keep = (strip_rows[:, None] >= global_col[None, :]) & (global_col[None, :] >= 2 * NB)
        masked = jnp.where(keep, adjoint_strip, 0.0)
        row_part = matmul(masked, by_col)
        col_total = col_total + tmatmul(masked, lax.dynamic_slice_in_dim(by_row, row_start, NB, 0))
        return col_total, row_part

    start_total = jnp.zeros((N, 2 * NB), jnp.float32)
    col_total, row_parts = lax.scan(one_block, start_total, jnp.arange(MB, dtype=jnp.int32))
    row_total = row_parts.reshape(N, 2 * NB)
    product = row_total[back_row] + col_total[back_col]

    l_second = jnp.tril(second_panel[NB:2 * NB])
    inv_second = inverse_lower(l_second)
    g_second = jnp.where(trailing, matmul(second_bar - product[:, NB:], inv_second), 0.0)
    k_second = jnp.tril(second_bar[NB:2 * NB]) - jnp.tril(tmatmul(g_second, panels[:, NB:]))
    e_second = diagonal_adjoint(l_second, k_second, inv_second)

    l_first = jnp.tril(first_panel[:NB])
    inv_first = inverse_lower(l_first)
    link_block = first_panel[NB:2 * NB]
    tail_rows = jnp.where(trailing, first_bar - product[:, :NB] - matmul(g_second, link_block), 0.0)
    head_rows = first_bar[NB:2 * NB] - matmul(e_second + e_second.T, link_block) - tmatmul(g_second, panels[:, :NB])
    residual = jnp.concatenate([jnp.zeros((NB, NB), jnp.float32), head_rows, tail_rows[2 * NB:]], 0)
    g_first = matmul(residual, inv_first)
    k_first = jnp.tril(first_bar[:NB]) - jnp.tril(tmatmul(g_first, first_panel))
    e_first = diagonal_adjoint(l_first, k_first, inv_first)

    left_half = jnp.concatenate([e_first, g_first[NB:]], 0)
    right_half = jnp.concatenate([jnp.zeros((NB, NB), jnp.float32), e_second, g_second[2 * NB:]], 0)
    whole = jnp.concatenate([left_half, right_half], 1)
    return whole[global_row]
```

```python
import jax
import jax.numpy as jnp
from jax import lax
from jax.experimental import pallas as pl
from jax.experimental.pallas import tpu as pltpu
from jax.sharding import PartitionSpec as P

NB = 256
HIGH = lax.Precision.HIGH
HIGHEST = lax.Precision.HIGHEST


def matmul(left, right):
    return jnp.dot(left, right, precision=HIGH, preferred_element_type=jnp.float32)


def tmatmul(left, right):
    return lax.dot_general(
        left, right, (((0,), (0,)), ((), ())), precision=HIGH, preferred_element_type=jnp.float32
    )


def dot(left, right):
    return jnp.dot(left, right, precision=HIGHEST, preferred_element_type=jnp.float32)


def tdot(left, right):
    return dot(left.T, right)


def positions():
    rows = lax.broadcasted_iota(jnp.int32, (NB, NB), 0)
    cols = lax.broadcasted_iota(jnp.int32, (NB, NB), 1)
    return rows, cols


def inverse_kernel(block_ref, out_ref):
    rows, cols = positions()
    block = block_ref[...]
    diagonal = rows == cols
    inverse = jnp.where(diagonal, 1.0 / jnp.where(diagonal, block, 1.0), 0.0)
    size = 1
    while size < NB:
        corner = (
            (rows // (2 * size) == cols // (2 * size))
            & (rows // size % 2 == 1)
            & (cols // size % 2 == 0)
        )
        inverse = inverse - dot(inverse, dot(jnp.where(corner, block, 0.0), inverse))
        size *= 2
    out_ref[...] = inverse


def inverse_lower(block):
    return pl.pallas_call(
        inverse_kernel,
        out_shape=jax.ShapeDtypeStruct((NB, NB), jnp.float32),
        name="inverse_lower",
        cost_estimate=pl.CostEstimate(
            flops=16 * 12 * NB**3, bytes_accessed=8 * NB * NB, transcendentals=0
        ),
    )(block)


def head_kernel(l0, l1, c, v0, v1, a00, a10, a11, z00, z10, z11, e0_ref, g0_ref, e1_ref):
    rows, cols = positions()

    def tril(x):
        return jnp.where(rows >= cols, x, 0.0)

    def phi(x):
        return jnp.where(rows > cols, x, jnp.where(rows == cols, 0.5 * x, 0.0))

    def diagonal_adjoint(block, block_bar, inverse_t, inverse):
        inner = phi(tdot(block, block_bar))
        s = dot(inverse_t, dot(inner, inverse))
        return phi(s + s.T)

    link = c[...]
    inv1, inv0 = v1[...], v0[...]
    inv1_t, inv0_t = inv1.T, inv0.T
    cross = dot(inv1_t, z10[...])
    k1 = tril(a11[...] - dot(inv1_t, z11[...]))
    e1 = diagonal_adjoint(tril(l1[...]), k1, inv1_t, inv1)
    rest = a10[...] - dot(e1 + e1.T, link) - cross
    g0_ref[...] = dot(rest, inv0)
    total = dot(inv0_t, z00[...] - tdot(link, cross) + tdot(rest, link))
    k0 = tril(a00[...] - total)
    e0_ref[...] = diagonal_adjoint(tril(l0[...]), k0, inv0_t, inv0)
    e1_ref[...] = e1


def head_blocks(*blocks):
    shape = jax.ShapeDtypeStruct((NB, NB), jnp.float32)
    return pl.pallas_call(
        head_kernel,
        out_shape=(shape, shape, shape),
        name="head_blocks",
        cost_estimate=pl.CostEstimate(
            flops=13 * 12 * NB**3, bytes_accessed=56 * NB * NB, transcendentals=0
        ),
    )(*blocks)


def local(factor, adjoint):
    n_rows = lax.axis_size("row")
    n_cols = lax.axis_size("col")
    n_pairs = n_cols // 2
    row_id = lax.axis_index("row")
    col_id = lax.axis_index("col")
    pair = col_id // 2
    lane = col_id % 2
    x_id = row_id % 2
    near = row_id // 2 == pair % 2
    local_rows, local_cols = factor.shape
    own_rows = local_rows // n_pairs

    def send(value, targets):
        edges = []
        for r in range(n_rows):
            for c in range(n_cols):
                target = targets(r, c // 2, c % 2)
                if target is not None:
                    edges.append((r * n_cols + c, target[0] * n_cols + target[1] * 2 + target[2]))
        return lax.ppermute(value, ("row", "col"), edges)

    def swap(value):
        return send(value, lambda r, p, k: (r, p, 1 - k))

    def rows_of(value, index, size):
        return lax.dynamic_slice_in_dim(value, index * size, size, 0)

    other = swap(adjoint)
    is_first = lane == 0
    whole = jnp.concatenate(
        [jnp.where(is_first, adjoint, other), jnp.where(is_first, other, adjoint)], 1
    )
    row_ids = jnp.arange(local_rows, dtype=jnp.int32)
    global_row = (row_ids // NB * n_rows + row_id) * NB + row_ids % NB
    col_ids = jnp.arange(local_cols, dtype=jnp.int32)
    global_col = (col_ids // NB * n_cols + 2 * pair) * NB + col_ids % NB
    global_col = jnp.concatenate([global_col, global_col + NB])
    trailing = (global_row >= 2 * NB)[:, None]
    masked = jnp.where(trailing & (global_row[:, None] >= global_col[None, :]), whole, 0.0)

    piece_rows = local_rows // 4
    panel = jnp.where(pair == 0, factor[:, :NB], 0.0)
    pieces = []
    for index in (3, 2, 1, 0):
        moving = factor[index * piece_rows : (index + 1) * piece_rows, :NB]
        arrived = panel[index * piece_rows : (index + 1) * piece_rows]
        for hop in range(1, n_pairs):
            moving = send(
                moving, lambda r, p, k, hop=hop: (r, hop, k) if p == hop - 1 else None
            )
            arrived = arrived + moving
        pieces.append(arrived)
    pieces = pieces[::-1]
    head = pieces[0][:NB]
    low = jnp.concatenate(pieces[:2], 0)
    low = jnp.where(trailing[: local_rows // 2], low, 0.0)
    high = jnp.concatenate(pieces[2:], 0)
    chosen_rows = jnp.concatenate([low, high], 0)

    def spread(value):
        def at(d):
            return send(
                value, lambda r, p, k: (r ^ d, p, k) if r // 2 == p % 2 else None
            )

        same = jnp.where(near, value, 0.0) + at(2)
        across = at(1) + at(3)
        return jnp.where(x_id == 0, same, across), jnp.where(x_id == 0, across, same)

    high_0, high_1 = spread(rows_of(high, pair // 2, NB))
    low_0, low_1 = spread(rows_of(low, pair // 2, NB))
    chosen_cols = jnp.concatenate([low_0, high_0, low_1, high_1], 0)

    def from_head(d):
        return send(head, lambda r, p, k: (r ^ d, p, k) if r < 2 else None)

    head_1, head_2, head_3 = from_head(1), from_head(2), from_head(3)

    def by_row(*values):
        result = values[3]
        for index in (2, 1, 0):
            result = jnp.where(row_id == index, values[index], result)
        return result

    top = by_row(head, head_1, head_2, head_3)
    link = by_row(head_1, head, head_3, head_2)
    inverse = inverse_lower(jnp.where(is_first, top, link))

    row_part = matmul(masked, chosen_cols)
    col_part = tmatmul(masked, chosen_rows)

    chosen_other = swap(chosen_rows)
    own_product = tmatmul(row_part, chosen_rows)
    other_product = tmatmul(row_part, chosen_other)
    first_pair = pair == 0
    own_term = jnp.where(is_first, col_part[:NB], col_part[2 * NB : 3 * NB])
    own_sum = jnp.where(first_pair, own_term, 0.0) - own_product - own_product.T
    other_sum = jnp.where(
        is_first,
        jnp.where(first_pair, col_part[2 * NB : 3 * NB], 0.0) - other_product.T,
        -other_product,
    )
    sums = jnp.concatenate([own_sum, other_sum], 0)
    slice_rows = 2 * NB // n_rows
    part = rows_of(sums, row_id, slice_rows)
    for d in range(1, n_rows):
        part = part + send(
            rows_of(sums, row_id ^ d, slice_rows), lambda r, p, k, d=d: (r ^ d, p, k)
        )
    total = part
    for source in range(1, n_pairs):
        total = total + send(
            part, lambda r, p, k, source=source: (r, 0, k) if p == source else None
        )
    gathered = [total] + [
        send(total, lambda r, p, k, d=d: (r ^ d, 0, k) if p == 0 and r ^ d < 2 else None)
        for d in range(1, n_rows)
    ]
    in_first_row = row_id == 0
    sums = jnp.where(
        in_first_row,
        jnp.concatenate(gathered, 0),
        jnp.concatenate([gathered[1], gathered[0], gathered[3], gathered[2]], 0),
    )

    remaining = jnp.where(first_pair, adjoint[:, :NB], 0.0) - row_part
    mine = rows_of(remaining, pair, own_rows)
    for d in range(1, n_pairs):
        mine = mine + send(
            rows_of(remaining, pair ^ d, own_rows), lambda r, p, k, d=d: (r, p ^ d, k)
        )
    half_rows = 2 * NB
    col_same = rows_of(col_part, x_id, half_rows)
    col_across = rows_of(col_part, 1 - x_id, half_rows)
    col_sum = (
        col_same
        + send(col_across, lambda r, p, k: (r ^ 1, p, k) if r // 2 == p % 2 else None)
        + send(col_same, lambda r, p, k: (r ^ 2, p, k) if r // 2 != p % 2 else None)
        + send(col_across, lambda r, p, k: (r ^ 3, p, k) if r // 2 != p % 2 else None)
    )
    for index in range(2):
        mine = mine - send(
            col_sum[index * NB : (index + 1) * NB],
            lambda r, p, k, index=index: (
                (r, p // 2 + index * (n_pairs // 2), k) if r // 2 == p % 2 else None
            ),
        )
    solved = matmul(mine, inverse)
    second = send(solved, lambda r, p, k: (r, p, 0) if k == 1 else None)
    solved = matmul(mine - matmul(second, link), inverse)

    bar = adjoint[:NB, :NB]
    bar_across = send(bar, lambda r, p, k: (r ^ 1, 0, k) if p == 0 and r < 2 else None)
    bar_top = jnp.where(in_first_row, bar, bar_across)
    bar_link = jnp.where(in_first_row, bar_across, bar)
    mine_head = jnp.concatenate([top, link, inverse, bar_top, bar_link], 0)
    their_head = swap(mine_head)
    their_sums = swap(sums)
    firsts = jnp.where(is_first, mine_head, their_head)
    seconds = jnp.where(is_first, their_head, mine_head)
    first_sums = jnp.where(is_first, sums, their_sums)
    second_sums = jnp.where(is_first, their_sums, sums)
    e_first, g_head, e_second = head_blocks(
        firsts[:NB],
        seconds[NB : 2 * NB],
        firsts[NB : 2 * NB],
        firsts[2 * NB : 3 * NB],
        seconds[2 * NB : 3 * NB],
        firsts[3 * NB : 4 * NB],
        firsts[4 * NB :],
        seconds[4 * NB :],
        first_sums[:NB],
        first_sums[NB:] + second_sums[NB:],
        second_sums[:NB],
    )
    leading = jnp.where(
        in_first_row,
        jnp.where(is_first, e_first, 0.0),
        jnp.where(is_first, g_head, e_second),
    )
    solved = jnp.where(first_pair & (row_id < 2), leading, solved)

    column = jnp.zeros((local_rows, NB), jnp.float32)
    column = lax.dynamic_update_slice_in_dim(column, solved, pair * own_rows, 0)
    for d in range(1, n_pairs):
        piece = send(solved, lambda r, p, k, d=d: (r, p ^ d, k))
        column = lax.dynamic_update_slice_in_dim(column, piece, (pair ^ d) * own_rows, 0)
    column_other = swap(column)
    return jnp.concatenate(
        [jnp.where(is_first, column, column_other), jnp.where(is_first, column_other, column)], 1
    )


def solution(mesh):
    placed = (P("row", "col"), P("row", "col"))
    return jax.shard_map(
        local, mesh=mesh, in_specs=placed, out_specs=P("row", None), check_vma=False
    )
```

```python
import functools

import jax
import jax.numpy as jnp
from jax import lax
from jax.experimental import pallas as pl
from jax.experimental.pallas import tpu as pltpu
from jax.sharding import PartitionSpec as P

NB = 256
ROW, PAIR, LANE = 0, 1, 2
SQUARE = jax.ShapeDtypeStruct((NB, NB), jnp.float32)


def dot(left, right):
    return jnp.dot(
        left, right, precision=lax.Precision.HIGHEST, preferred_element_type=jnp.float32
    )


def split(value):
    high = value.astype(jnp.bfloat16)
    return high, (value - high.astype(jnp.float32)).astype(jnp.bfloat16)


def dot3(left, right):
    once = functools.partial(jnp.dot, preferred_element_type=jnp.float32)
    return once(left[0], right[0]) + (once(left[0], right[1]) + once(left[1], right[0]))


def quick(left, right):
    return dot3(split(left), split(right))


def positions():
    rows = lax.broadcasted_iota(jnp.int32, (NB, NB), 0)
    cols = lax.broadcasted_iota(jnp.int32, (NB, NB), 1)
    return rows, cols


def call(kernel, name, out_shape, ids, *arrays, scratch=()):
    sizes = [x.size * x.dtype.itemsize for x in (*arrays, *jax.tree.leaves(out_shape))]
    return pl.pallas_call(
        kernel,
        out_shape=out_shape,
        in_specs=[pl.BlockSpec(memory_space=pltpu.SMEM)]
        + [pl.BlockSpec(memory_space=pltpu.VMEM)] * len(arrays),
        scratch_shapes=list(scratch),
        name=name,
        cost_estimate=pl.CostEstimate(flops=1, bytes_accessed=1, transcendentals=0),
        compiler_params=pltpu.CompilerParams(vmem_limit_bytes=min(60, 16 + sum(sizes) // 2**19) * 2**20),
    )(ids, *arrays)


def inverse_kernel(ids, block_ref, out_ref):
    @pl.when((ids[PAIR] == 0) & (ids[ROW] < 2))
    def _():
        half = NB // 2
        rows = lax.broadcasted_iota(jnp.int32, (half, half), 0)
        cols = lax.broadcasted_iota(jnp.int32, (half, half), 1)
        blocks = [block_ref[:half, :half], block_ref[half:, half:]]
        diagonal = rows == cols
        inverses = [
            jnp.where(diagonal, 1.0 / jnp.where(diagonal, x, 1.0), 0.0) for x in blocks
        ]
        size = 1
        while size < half:
            corner = (
                (rows // (2 * size) == cols // (2 * size))
                & (rows // size % 2 == 1)
                & (cols // size % 2 == 0)
            )
            inner = [dot(jnp.where(corner, x, 0.0), y) for x, y in zip(blocks, inverses)]
            inverses = [y - dot(y, x) for x, y in zip(inner, inverses)]
            size *= 2
        out_ref[:half, :half] = inverses[0]
        out_ref[:half, half:] = jnp.zeros((half, half), jnp.float32)
        out_ref[half:, half:] = inverses[1]
        out_ref[half:, :half] = -dot(inverses[1], dot(block_ref[half:, :half], inverses[0]))

    @pl.when((ids[PAIR] != 0) | (ids[ROW] >= 2))
    def _():
        out_ref[...] = jnp.zeros_like(out_ref)


def mask_kernel(n_rows, n_cols, ids, own, other, low_1, low_2, high_1, high_2):
    rows, cols = positions()
    below = rows - cols
    first = ids[LANE] == 0
    blocks = own.shape[0] // NB

    def masked(index, half, core):
        at = pl.ds(pl.multiple_of(index * NB, NB), NB)
        columns = slice(half * NB, (half + 1) * NB)
        mine = first if core == 0 else jnp.logical_not(first)
        value = jnp.where(mine, own[at, columns], other[at, columns])
        row_block = index * n_rows + ids[ROW]
        col_block = 2 * ids[PAIR] + half * n_cols + core
        least = jnp.where(row_block > col_block, -NB, jnp.where(row_block == col_block, 0, NB))
        least = jnp.where(row_block >= 2, least, NB)
        return split(jnp.where(below >= least, value, 0.0))

    @pl.loop(0, blocks)
    def _(index):
        for core in range(2):
            columns = slice(core * NB, (core + 1) * NB)
            at = pl.ds(pl.multiple_of(index * NB, NB), NB)
            low_1[at, columns], low_2[at, columns] = masked(index, 0, core)

    @pl.loop(0, blocks // 2)
    def _(index):
        for core in range(2):
            columns = slice(core * NB, (core + 1) * NB)
            at = pl.ds(pl.multiple_of(index * NB, NB), NB)
            high_1[at, columns], high_2[at, columns] = masked(index + blocks // 2, 1, core)


def column_kernel(n_rows, ids, low_1, low_2, high_1, high_2, *refs):
    refs, turned, low_ref, targets, sums = refs[:-7], refs[-7], refs[-6], refs[-5:-1], refs[-1]
    blocks = low_1.shape[0] // NB
    per_piece = blocks // 4
    low = jnp.zeros((NB, 2 * NB), jnp.float32)
    high = jnp.zeros((NB, 2 * NB), jnp.float32)
    for index, piece in enumerate(refs):
        for inner in range(per_piece):
            block = index * per_piece + inner
            at = slice(inner * NB, (inner + 1) * NB)
            value = piece[at, :]
            if block == 0:
                value = jnp.where(ids[ROW] >= 2, value, 0.0)
            value = value.T
            turned[:, block * NB : (block + 1) * NB] = value
            value = split(value)
            at = slice(block * NB, (block + 1) * NB)
            low += dot3(value, (low_1[at, :], low_2[at, :]))
            if block >= blocks // 2:
                block -= blocks // 2
                at = slice(block * NB, (block + 1) * NB)
                high += dot3(value, (high_1[at, :], high_2[at, :]))
    low_ref[...] = low
    sums[0], sums[1], sums[2], sums[3] = low[:, :NB], low[:, NB:], high[:, :NB], high[:, NB:]
    for d in range(n_rows):
        target = ids[ROW] ^ d
        targets[d][...] = sums[jnp.where(target // 2 == ids[PAIR] % 2, 0, 2) + target % 2]


def row_kernel(n_pairs, n_rows, ids, low_1, low_2, high_1, high_2, *refs):
    held, (turned, turned_other, adjoint, low), columns = refs[:4], refs[4:8], refs[8:12]
    shares, slices = refs[12 : 12 + n_pairs], refs[12 + n_pairs : 12 + n_pairs + n_rows]
    remaining, sums = refs[-2:]
    pair, row = ids[PAIR], ids[ROW]
    x_is_0 = row % 2 == 0
    near = row // 2 == pair % 2
    first = ids[LANE] == 0

    def panel(same, across):
        return split(
            jnp.concatenate(
                [jnp.where(x_is_0, same, across), jnp.where(x_is_0, across, same)], 0
            )
        )

    v0, v1, v2, v3 = [ref[...] for ref in held]
    panel_low = panel(jnp.where(near, v0, v2), jnp.where(near, v1, v3))
    panel_high = panel(jnp.where(near, v2, v0), jnp.where(near, v3, v1))
    own = jnp.zeros((NB, NB), jnp.float32)
    other = jnp.zeros((NB, NB), jnp.float32)
    for block in range(n_pairs):
        at = slice(block * NB, (block + 1) * NB)
        product = dot3((low_1[at, :], low_2[at, :]), panel_low)
        if block >= n_pairs // 2:
            upper = slice((block - n_pairs // 2) * NB, (block - n_pairs // 2 + 1) * NB)
            product += dot3((high_1[upper, :], high_2[upper, :]), panel_high)
        remaining[block] = jnp.where(pair == 0, adjoint[at, :NB], 0.0) - product
        product = split(product)
        own += dot3(split(turned[:, at]), product)
        other += dot3(split(turned_other[:, at]), product)
    for d in range(n_pairs):
        shares[d][...] = remaining[pair ^ d]
    first_pair = pair == 0
    own_term = jnp.where(first, low[:, :NB], low[:, NB:])
    own_term = jnp.where(first_pair, own_term, 0.0)
    cross_term = jnp.where(first_pair, low[:, NB:], 0.0)
    own_sum = (own_term - own).T - own
    other_sum = jnp.where(first, cross_term.T - other, -other.T)
    height = 2 * NB // n_rows
    for index in range(n_rows // 2):
        at = slice(index * height, (index + 1) * height)
        sums[index] = own_sum[at]
        sums[index + n_rows // 2] = other_sum[at]
    for d in range(n_rows):
        slices[d][:NB, :] = columns[d][...]
        slices[d][NB:, :] = sums[row ^ d]


def by_row(row, values):
    result = values[3]
    for index in (2, 1, 0):
        result = jnp.where(row == index, values[index], result)
    return result


def carried_blocks(ids, refs):
    values = [ref[...] for ref in refs]
    top = by_row(ids[ROW], values)
    link = by_row(ids[ROW], [values[1], values[0], values[3], values[2]])
    return jnp.where(ids[LANE] == 0, top, link), link


def solve_kernel(n_pairs, ids, *refs):
    shares, owned, carried = refs[:n_pairs], refs[n_pairs], refs[n_pairs + 1 : -2]
    total_ref, solved = refs[-2:]
    total = shares[0][...]
    for ref in shares[1:]:
        total = total + ref[...]
    total = total - owned[...].T
    inverse, _ = carried_blocks(ids, carried)
    total_ref[...] = total
    solved[:NB, :] = quick(total, inverse)
    solved[NB:, :] = inverse


def end_kernel(ids, total, solved, second, c0, c1, c2, c3, blocks, across, blocks_other, across_other, sums_ref, sums_other, out_ref):
    row, first = ids[ROW], ids[LANE] == 0
    leading = (ids[PAIR] == 0) & (row < 2)

    @pl.when(jnp.logical_not(leading))
    def _():
        inverse, link = carried_blocks(ids, (c0, c1, c2, c3))
        whole = quick(total[...] - quick(second[:NB, :], link), inverse)
        out_ref[...] = jnp.where(first, whole, solved[:NB, :])

    @pl.when(leading)
    def _():
        rows, cols = positions()
        in_first_row = row == 0

        def tril(x):
            return jnp.where(rows >= cols, x, 0.0)

        def phi(x):
            return jnp.where(rows > cols, x, jnp.where(rows == cols, 0.5 * x, 0.0))

        def diagonal_adjoint(block, block_bar, inverse_t, inverse):
            inner = phi(quick(block.T, block_bar))
            s = quick(inverse_t, quick(inner, inverse))
            return phi(s + s.T)

        def by_lane(own, other):
            return jnp.where(first, own, other), jnp.where(first, other, own)

        def held(own, other):
            firsts, seconds = by_lane(own[...], other[...])
            return [x[i * NB : (i + 1) * NB] for x in (firsts, seconds) for i in range(2)]

        mine, theirs = held(blocks, blocks_other), held(across, across_other)
        l0, a00, _, _ = [jnp.where(in_first_row, a, b) for a, b in zip(mine, theirs)]
        link, a10, l1, a11 = [jnp.where(in_first_row, b, a) for a, b in zip(mine, theirs)]
        inv0, inv1 = by_lane(solved[NB:, :], second[NB:, :])

        def ordered(ref):
            value = ref[...]
            height = value.shape[0] // 4
            parts = [value[i * height : (i + 1) * height] for i in range(4)]
            swapped = jnp.concatenate([parts[1], parts[0], parts[3], parts[2]], 0)
            return jnp.where(in_first_row, value, swapped)

        sums_0, sums_1 = by_lane(ordered(sums_ref), ordered(sums_other))
        z00, z11, z10 = sums_0[:NB], sums_1[:NB], sums_0[NB:] + sums_1[NB:]
        inv1_t, inv0_t = inv1.T, inv0.T
        cross = quick(inv1_t, z10)
        k1 = tril(a11 - quick(inv1_t, z11))
        e1 = diagonal_adjoint(tril(l1), k1, inv1_t, inv1)
        rest = a10 - quick(e1 + e1.T, link) - cross
        g0 = quick(rest, inv0)
        k0 = tril(a00 - quick(inv0_t, z00 - quick(link.T, cross) + quick(rest.T, link)))
        e0 = diagonal_adjoint(tril(l0), k0, inv0_t, inv0)
        out_ref[...] = jnp.where(
            in_first_row, jnp.where(first, e0, 0.0), jnp.where(first, g0, e1)
        )


def place_kernel(n_pairs, ids, *refs):
    own, other, out_ref = refs[:n_pairs], refs[n_pairs:-1], refs[-1]
    first = ids[LANE] == 0
    for d in range(n_pairs):
        at = pl.ds(pl.multiple_of((ids[PAIR] ^ d) * NB, NB), NB)
        mine, theirs = own[d][...], other[d][...]
        out_ref[at, :NB] = jnp.where(first, mine, theirs)
        out_ref[at, NB:] = jnp.where(first, theirs, mine)


def after(value, *earlier):
    return lax.optimization_barrier((value, *earlier))[0]


def together(*values):
    return lax.optimization_barrier(values)


def local(factor, adjoint):
    n_rows = lax.axis_size("row")
    n_cols = lax.axis_size("col")
    n_pairs = n_cols // 2
    row_id = lax.axis_index("row")
    col_id = lax.axis_index("col")
    pair = col_id // 2
    lane = col_id % 2
    ids = jnp.stack([row_id, pair, lane])
    near = row_id // 2 == pair % 2
    first_pair = pair == 0
    local_rows = factor.shape[0]
    piece_rows = local_rows // 4

    def send(value, targets):
        edges = []
        for r in range(n_rows):
            for c in range(n_cols):
                target = targets(r, c // 2, c % 2)
                if target is not None:
                    edges.append((r * n_cols + c, target[0] * n_cols + target[1] * 2 + target[2]))
        return lax.ppermute(value, ("row", "col"), edges)

    def swap(value):
        return send(value, lambda r, p, k: (r, p, 1 - k))

    def swap_rows(value, d):
        return send(value, lambda r, p, k: (r ^ d, p, k))

    def swap_pairs(value, d):
        return send(value, lambda r, p, k: (r, p ^ d, k))

    panel = together(
        *[factor[i * piece_rows : (i + 1) * piece_rows, :NB] for i in range(4)], factor[:NB, :NB]
    )
    corner = panel[-1]

    def hop(value, number):
        return send(value, lambda r, p, k: (r, number, k) if p == number - 1 else None)

    def travel(value, hops):
        arrived = [value]
        for number in hops:
            arrived.append(hop(arrived[-1], number))
        return arrived

    def here(arrived):
        value = arrived[0]
        for p in range(1, len(arrived)):
            value = jnp.where(pair == p, arrived[p], value)
        return value

    middle = n_pairs // 2
    row_ids = jnp.arange(piece_rows, dtype=jnp.int32)
    trailing = ((row_ids >= NB) | (row_id >= 2))[:, None]

    def chosen(nearer, farther):
        start = pair // 2 % (piece_rows // NB) * NB
        value = here(nearer[:middle] + farther[middle:])
        return lax.dynamic_slice_in_dim(value, start, NB, 0)

    own_inverse = call(inverse_kernel, "inverse", SQUARE, ids, corner)
    carried = jnp.where((row_id == 1) & (lane == 0), corner, own_inverse)
    leading_piece = jnp.where(
        row_id < 2, jnp.concatenate([carried, panel[0][NB:]], 0), panel[0]
    )
    blocks = jnp.concatenate([corner, adjoint[:NB, :NB]], 0)
    across = send(blocks, lambda r, p, k: (r ^ 1, p, k) if p == 0 and r < 2 else None)
    every, nearest = range(1, n_pairs), range(1, middle)
    arrived_3, arrived_1, arrived_2 = [travel(panel[i], every) for i in (3, 1, 2)]
    arrived_0 = travel(leading_piece, nearest)
    high = swap_rows(chosen(arrived_2, arrived_3), 2)
    high, across, blocks, *rest = together(high, across, blocks, *arrived_3, *arrived_1, *arrived_2, *arrived_0)
    arrived_3, rest = rest[:n_pairs], rest[n_pairs:]
    arrived_1, rest = rest[:n_pairs], rest[n_pairs:]
    arrived_2, arrived_0 = rest[:n_pairs], rest[n_pairs:]

    masked_0 = [jnp.where(trailing, x, 0.0) for x in arrived_0]
    low = chosen(masked_0, arrived_1)
    held = jnp.where(near, low, high)
    held = [held] + [swap_rows(held, d) for d in range(1, n_rows)]
    carried = [x[:NB] for x in arrived_0]
    carried = carried + travel(carried[-1], range(middle, n_pairs))[1:]
    columns = jax.ShapeDtypeStruct((local_rows, 2 * NB), jnp.bfloat16)
    half_columns = jax.ShapeDtypeStruct((local_rows // 2, 2 * NB), jnp.bfloat16)
    masked = call(
        functools.partial(mask_kernel, n_rows, n_cols),
        "masked",
        (columns, columns, half_columns, half_columns),
        ids,
        adjoint,
        swap(after(adjoint, high)),
    )
    pieces = here(masked_0), here(arrived_1), here(arrived_2), here(arrived_3)
    rest = together(*held, *masked, *pieces, *carried)
    held, masked, pieces, carried = rest[:4], rest[4:8], rest[8:12], here(rest[12:])

    turned, low, *block_sums = call(
        functools.partial(column_kernel, n_rows),
        "columns",
        (
            jax.ShapeDtypeStruct((NB, local_rows), jnp.float32),
            jax.ShapeDtypeStruct((NB, 2 * NB), jnp.float32),
        )
        + (SQUARE,) * n_rows,
        ids,
        *masked,
        *pieces,
        scratch=(pltpu.VMEM((4, NB, NB), jnp.float32),),
    )

    height = 2 * NB // n_rows
    rows = call(
        functools.partial(row_kernel, n_pairs, n_rows),
        "rows",
        (SQUARE,) * n_pairs
        + (jax.ShapeDtypeStruct((NB + height, NB), jnp.float32),) * n_rows,
        ids,
        *masked,
        *held,
        turned,
        swap(turned),
        adjoint,
        low,
        *block_sums,
        scratch=(
            pltpu.VMEM((n_pairs, NB, NB), jnp.float32),
            pltpu.VMEM((n_rows, height, NB), jnp.float32),
        ),
    )
    carried = [carried] + [swap_rows(carried, d) for d in range(1, n_rows)]
    rest = together(*carried, *rows)
    carried, rows = rest[:n_rows], rest[n_rows:]
    shares, slices = rows[:n_pairs], rows[n_pairs:]

    farther_shares = [swap_pairs(shares[d], d) for d in range(2, n_pairs)]
    slices = [slices[0]] + [swap_rows(slices[d], d) for d in range(1, n_rows)]
    next_share, *rest = together(shares[1], *farther_shares, *slices)
    farther_shares, slices = rest[: n_pairs - 2], rest[n_pairs - 2 :]
    slices = sum(slices[1:], slices[0])

    def owner(r, p, k):
        half = 0 if r // 2 == p % 2 else 1
        return p % 2 * 2 + r % 2, p // 2 + half * (n_pairs // 2), k

    owned = send(slices[:NB], owner)
    total = slices[NB:]
    totals = [total] + [swap_pairs(total, d) for d in range(1, n_pairs)]
    next_share = swap_pairs(next_share, 1)
    owned, next_share, *totals = together(owned, next_share, *totals)
    shares = [shares[0], next_share, *farther_shares]

    mine, solved = call(
        functools.partial(solve_kernel, n_pairs),
        "solve",
        (SQUARE, jax.ShapeDtypeStruct((2 * NB, NB), jnp.float32)),
        ids,
        *shares,
        owned,
        *carried,
    )
    total = sum(totals[1:], totals[0])
    sums = [total] + [swap_rows(total, d) for d in range(1, n_rows)]
    second = swap(solved)
    blocks_other = swap(after(blocks, solved))
    second, blocks_other, *sums = together(second, blocks_other, *sums)
    across_other = swap(after(across, second))
    sums = jnp.concatenate(sums, 0)
    result = call(
        end_kernel,
        "end",
        SQUARE,
        ids,
        mine,
        solved,
        second,
        *carried,
        blocks,
        across,
        blocks_other,
        across_other,
        sums,
        swap(sums),
    )
    results = [result] + [swap_pairs(result, d) for d in range(1, n_pairs)]
    return call(
        functools.partial(place_kernel, n_pairs),
        "place",
        jax.ShapeDtypeStruct((local_rows, 2 * NB), jnp.float32),
        ids,
        *results,
        *[swap(x) for x in results],
    )


def solution(mesh):
    placed = (P("row", "col"), P("row", "col"))
    return jax.shard_map(
        local, mesh=mesh, in_specs=placed, out_specs=P("row", None), check_vma=False
    )
```

```python
import functools

import jax
import jax.numpy as jnp
from jax import lax
from jax.experimental import pallas as pl
from jax.experimental.pallas import tpu as pltpu
from jax.sharding import PartitionSpec as P

NB = 256
ROW, PAIR, LANE = 0, 1, 2
SQUARE = jax.ShapeDtypeStruct((NB, NB), jnp.float32)


def dot(left, right):
    return jnp.dot(
        left, right, precision=lax.Precision.HIGHEST, preferred_element_type=jnp.float32
    )


def split(value):
    high = value.astype(jnp.bfloat16)
    return high, (value - high.astype(jnp.float32)).astype(jnp.bfloat16)


def dot3(left, right):
    once = functools.partial(jnp.dot, preferred_element_type=jnp.float32)
    return once(left[0], right[0]) + (once(left[0], right[1]) + once(left[1], right[0]))


def quick(left, right):
    return dot3(split(left), split(right))


def positions():
    rows = lax.broadcasted_iota(jnp.int32, (NB, NB), 0)
    cols = lax.broadcasted_iota(jnp.int32, (NB, NB), 1)
    return rows, cols


def call(kernel, name, out_shape, ids, *arrays, scratch=()):
    sizes = [x.size * x.dtype.itemsize for x in (*arrays, *jax.tree.leaves(out_shape))]
    return pl.pallas_call(
        kernel,
        out_shape=out_shape,
        in_specs=[pl.BlockSpec(memory_space=pltpu.SMEM)]
        + [pl.BlockSpec(memory_space=pltpu.VMEM)] * len(arrays),
        scratch_shapes=list(scratch),
        name=name,
        cost_estimate=pl.CostEstimate(flops=1, bytes_accessed=1, transcendentals=0),
        compiler_params=pltpu.CompilerParams(vmem_limit_bytes=min(60, 16 + sum(sizes) // 2**19) * 2**20),
    )(ids, *arrays)


def inverse_kernel(ids, block_ref, out_ref):
    @pl.when((ids[PAIR] == 0) & (ids[ROW] < 2))
    def _():
        half = NB // 2
        rows = lax.broadcasted_iota(jnp.int32, (half, half), 0)
        cols = lax.broadcasted_iota(jnp.int32, (half, half), 1)
        blocks = [block_ref[:half, :half], block_ref[half:, half:]]
        diagonal = rows == cols
        inverses = [
            jnp.where(diagonal, 1.0 / jnp.where(diagonal, x, 1.0), 0.0) for x in blocks
        ]
        size = 1
        while size < half:
            corner = (
                (rows // (2 * size) == cols // (2 * size))
                & (rows // size % 2 == 1)
                & (cols // size % 2 == 0)
            )
            inner = [dot(jnp.where(corner, x, 0.0), y) for x, y in zip(blocks, inverses)]
            inverses = [y - dot(y, x) for x, y in zip(inner, inverses)]
            size *= 2
        out_ref[:half, :half] = inverses[0]
        out_ref[:half, half:] = jnp.zeros((half, half), jnp.float32)
        out_ref[half:, half:] = inverses[1]
        out_ref[half:, :half] = -dot(inverses[1], dot(block_ref[half:, :half], inverses[0]))

    @pl.when((ids[PAIR] != 0) | (ids[ROW] >= 2))
    def _():
        out_ref[...] = jnp.zeros_like(out_ref)


def mask_kernel(n_rows, n_cols, ids, own, other, low_1, low_2, high_1, high_2):
    rows, cols = positions()
    below = rows - cols
    first = ids[LANE] == 0
    blocks = own.shape[0] // NB

    def masked(index, half, core):
        at = pl.ds(pl.multiple_of(index * NB, NB), NB)
        columns = slice(half * NB, (half + 1) * NB)
        mine = first if core == 0 else jnp.logical_not(first)
        value = jnp.where(mine, own[at, columns], other[at, columns])
        row_block = index * n_rows + ids[ROW]
        col_block = 2 * ids[PAIR] + half * n_cols + core
        least = jnp.where(row_block > col_block, -NB, jnp.where(row_block == col_block, 0, NB))
        least = jnp.where(row_block >= 2, least, NB)
        return split(jnp.where(below >= least, value, 0.0))

    @pl.loop(0, blocks)
    def _(index):
        for core in range(2):
            columns = slice(core * NB, (core + 1) * NB)
            at = pl.ds(pl.multiple_of(index * NB, NB), NB)
            low_1[at, columns], low_2[at, columns] = masked(index, 0, core)

    @pl.loop(0, blocks // 2)
    def _(index):
        for core in range(2):
            columns = slice(core * NB, (core + 1) * NB)
            at = pl.ds(pl.multiple_of(index * NB, NB), NB)
            high_1[at, columns], high_2[at, columns] = masked(index + blocks // 2, 1, core)


def column_kernel(n_rows, ids, low_1, low_2, high_1, high_2, *refs):
    refs, turned, low_ref, targets, sums = refs[:-7], refs[-7], refs[-6], refs[-5:-1], refs[-1]
    blocks = low_1.shape[0] // NB
    per_piece = blocks // 4
    low = jnp.zeros((NB, 2 * NB), jnp.float32)
    high = jnp.zeros((NB, 2 * NB), jnp.float32)
    for index, piece in enumerate(refs):
        for inner in range(per_piece):
            block = index * per_piece + inner
            at = slice(inner * NB, (inner + 1) * NB)
            value = piece[at, :]
            if block == 0:
                value = jnp.where(ids[ROW] >= 2, value, 0.0)
            value = value.T
            turned[:, block * NB : (block + 1) * NB] = value
            value = split(value)
            at = slice(block * NB, (block + 1) * NB)
            low += dot3(value, (low_1[at, :], low_2[at, :]))
            if block >= blocks // 2:
                block -= blocks // 2
                at = slice(block * NB, (block + 1) * NB)
                high += dot3(value, (high_1[at, :], high_2[at, :]))
    low_ref[...] = low
    sums[0], sums[1], sums[2], sums[3] = low[:, :NB], low[:, NB:], high[:, :NB], high[:, NB:]
    for d in range(n_rows):
        target = ids[ROW] ^ d
        targets[d][...] = sums[jnp.where(target // 2 == ids[PAIR] % 2, 0, 2) + target % 2]


def row_kernel(n_pairs, ids, low_1, low_2, high_1, high_2, v0, v1, v2, v3, adjoint, *refs):
    shares, product_ref, remaining = refs[:n_pairs], refs[-2], refs[-1]
    pair, row = ids[PAIR], ids[ROW]
    x_is_0 = row % 2 == 0
    near = row // 2 == pair % 2

    def panel(same, across):
        return split(
            jnp.concatenate(
                [jnp.where(x_is_0, same, across), jnp.where(x_is_0, across, same)], 0
            )
        )

    v0, v1, v2, v3 = [ref[...] for ref in (v0, v1, v2, v3)]
    panel_low = panel(jnp.where(near, v0, v2), jnp.where(near, v1, v3))
    panel_high = panel(jnp.where(near, v2, v0), jnp.where(near, v3, v1))
    for block in range(n_pairs):
        at = slice(block * NB, (block + 1) * NB)
        product = dot3((low_1[at, :], low_2[at, :]), panel_low)
        if block >= n_pairs // 2:
            upper = slice((block - n_pairs // 2) * NB, (block - n_pairs // 2 + 1) * NB)
            product += dot3((high_1[upper, :], high_2[upper, :]), panel_high)
        remaining[block] = jnp.where(pair == 0, adjoint[at, :NB], 0.0) - product
        product_ref[at, :] = product
    for d in range(n_pairs):
        shares[d][...] = remaining[pair ^ d]


def sum_kernel(n_rows, ids, turned, turned_other, product_ref, low, *refs):
    slices, sums = refs[:-1], refs[-1]
    first, first_pair = ids[LANE] == 0, ids[PAIR] == 0
    own = jnp.zeros((NB, NB), jnp.float32)
    other = jnp.zeros((NB, NB), jnp.float32)
    for block in range(turned.shape[1] // NB):
        at = slice(block * NB, (block + 1) * NB)
        product = split(product_ref[at, :])
        own += dot3(split(turned[:, at]), product)
        other += dot3(split(turned_other[:, at]), product)
    own_term = jnp.where(first, low[:, :NB], low[:, NB:])
    own_term = jnp.where(first_pair, own_term, 0.0)
    cross_term = jnp.where(first_pair, low[:, NB:], 0.0)
    own_sum = (own_term - own).T - own
    other_sum = jnp.where(first, cross_term.T - other, -other.T)
    height = 2 * NB // n_rows
    for index in range(n_rows // 2):
        at = slice(index * height, (index + 1) * height)
        sums[index] = own_sum[at]
        sums[index + n_rows // 2] = other_sum[at]
    for d in range(n_rows):
        slices[d][...] = sums[ids[ROW] ^ d]


def carried_blocks(ids, refs):
    same, other = [ref[...] for ref in refs]
    even = ids[ROW] % 2 == 0
    link = jnp.where(even, other, same)
    return jnp.where(ids[LANE] == 0, jnp.where(even, same, other), link), link


def solve_kernel(n_pairs, ids, *refs):
    shares, owned, carried = refs[:n_pairs], refs[n_pairs], refs[n_pairs + 1 : -2]
    total_ref, solved = refs[-2:]
    total = shares[0][...]
    for ref in shares[1:]:
        total = total + ref[...]
    total = total - owned[...].T
    inverse, _ = carried_blocks(ids, carried)
    total_ref[...] = total
    solved[...] = quick(total, inverse)


def lead_kernel(ids, c0, c1, c0_other, c1_other, blocks, across, blocks_other, across_other, sums_ref, sums_other, out_ref):
    row, first = ids[ROW], ids[LANE] == 0
    own, other = (c0, c1), (c0_other, c1_other)

    @pl.when((ids[PAIR] == 0) & (row < 2))
    def _():
        rows, cols = positions()
        in_first_row = row == 0

        def tril(x):
            return jnp.where(rows >= cols, x, 0.0)

        def phi(x):
            return jnp.where(rows > cols, x, jnp.where(rows == cols, 0.5 * x, 0.0))

        def diagonal_adjoint(block, block_bar, inverse_t, inverse):
            inner = phi(quick(block.T, block_bar))
            s = quick(inverse_t, quick(inner, inverse))
            return phi(s + s.T)

        def by_lane(own, other):
            return jnp.where(first, own, other), jnp.where(first, other, own)

        def held(own, other):
            firsts, seconds = by_lane(own[...], other[...])
            return [x[i * NB : (i + 1) * NB] for x in (firsts, seconds) for i in range(2)]

        mine, theirs = held(blocks, blocks_other), held(across, across_other)
        l0, a00, _, _ = [jnp.where(in_first_row, a, b) for a, b in zip(mine, theirs)]
        link, a10, l1, a11 = [jnp.where(in_first_row, b, a) for a, b in zip(mine, theirs)]
        inv0, _ = by_lane(*[jnp.where(in_first_row, x[...], y[...]) for x, y in (own, other)])
        _, inv1 = by_lane(*[jnp.where(in_first_row, y[...], x[...]) for x, y in (own, other)])

        def ordered(ref):
            value = ref[...]
            height = value.shape[0] // 4
            parts = [value[i * height : (i + 1) * height] for i in range(4)]
            swapped = jnp.concatenate([parts[1], parts[0], parts[3], parts[2]], 0)
            return jnp.where(in_first_row, value, swapped)

        sums_0, sums_1 = by_lane(ordered(sums_ref), ordered(sums_other))
        z00, z11, z10 = sums_0[:NB], sums_1[:NB], sums_0[NB:] + sums_1[NB:]
        inv1_t, inv0_t = inv1.T, inv0.T
        cross = quick(inv1_t, z10)
        k1 = tril(a11 - quick(inv1_t, z11))
        e1 = diagonal_adjoint(tril(l1), k1, inv1_t, inv1)
        rest = a10 - quick(e1 + e1.T, link) - cross
        g0 = quick(rest, inv0)
        k0 = tril(a00 - quick(inv0_t, z00 - quick(link.T, cross) + quick(rest.T, link)))
        e0 = diagonal_adjoint(tril(l0), k0, inv0_t, inv0)
        out_ref[...] = jnp.where(
            in_first_row, jnp.where(first, e0, 0.0), jnp.where(first, g0, e1)
        )


def end_kernel(ids, total, solved, second, c0, c1, lead, out_ref):
    inverse, link = carried_blocks(ids, (c0, c1))
    whole = quick(total[...] - quick(second[...], link), inverse)
    whole = jnp.where(ids[LANE] == 0, whole, solved[...])
    out_ref[...] = jnp.where((ids[PAIR] == 0) & (ids[ROW] < 2), lead[...], whole)


def place_kernel(n_pairs, ids, *refs):
    own, other, out_ref = refs[:n_pairs], refs[n_pairs:-1], refs[-1]
    first = ids[LANE] == 0
    for d in range(n_pairs):
        at = pl.ds(pl.multiple_of((ids[PAIR] ^ d) * NB, NB), NB)
        mine, theirs = own[d][...], other[d][...]
        out_ref[at, :NB] = jnp.where(first, mine, theirs)
        out_ref[at, NB:] = jnp.where(first, theirs, mine)


def after(value, *earlier):
    return lax.optimization_barrier((value, *earlier))[0]


def together(*values):
    return lax.optimization_barrier(values)


def local(factor, adjoint):
    n_rows = lax.axis_size("row")
    n_cols = lax.axis_size("col")
    n_pairs = n_cols // 2
    row_id = lax.axis_index("row")
    col_id = lax.axis_index("col")
    pair = col_id // 2
    lane = col_id % 2
    ids = jnp.stack([row_id, pair, lane])
    near = row_id // 2 == pair % 2
    first_pair = pair == 0
    local_rows = factor.shape[0]
    piece_rows = local_rows // 4

    def send(value, targets):
        edges = []
        for r in range(n_rows):
            for c in range(n_cols):
                target = targets(r, c // 2, c % 2)
                if target is not None:
                    edges.append((r * n_cols + c, target[0] * n_cols + target[1] * 2 + target[2]))
        return lax.ppermute(value, ("row", "col"), edges)

    def swap(value):
        return send(value, lambda r, p, k: (r, p, 1 - k))

    def swap_rows(value, d):
        return send(value, lambda r, p, k: (r ^ d, p, k))

    def swap_pairs(value, d):
        return send(value, lambda r, p, k: (r, p ^ d, k))

    panel = together(
        *[factor[i * piece_rows : (i + 1) * piece_rows, :NB] for i in range(4)], factor[:NB, :NB]
    )
    corner = panel[-1]

    def hop(value, number):
        return send(value, lambda r, p, k: (r, number, k) if p == number - 1 else None)

    def travel(value, hops):
        arrived = [value]
        for number in hops:
            arrived.append(hop(arrived[-1], number))
        return arrived

    def here(arrived):
        value = arrived[0]
        for p in range(1, len(arrived)):
            value = jnp.where(pair == p, arrived[p], value)
        return value

    middle = n_pairs // 2
    row_ids = jnp.arange(piece_rows, dtype=jnp.int32)
    trailing = ((row_ids >= NB) | (row_id >= 2))[:, None]

    def chosen(nearer, farther):
        start = pair // 2 % (piece_rows // NB) * NB
        value = here(nearer[:middle] + farther[middle:])
        return lax.dynamic_slice_in_dim(value, start, NB, 0)

    own_inverse = call(inverse_kernel, "inverse", SQUARE, ids, corner)
    carried = jnp.where((row_id == 1) & (lane == 0), corner, own_inverse)
    leading_piece = jnp.where(
        row_id < 2, jnp.concatenate([carried, panel[0][NB:]], 0), panel[0]
    )
    blocks = jnp.concatenate([corner, adjoint[:NB, :NB]], 0)
    across = send(blocks, lambda r, p, k: (r ^ 1, p, k) if p == 0 and r < 2 else None)
    every, nearest = range(1, n_pairs), range(1, middle)
    arrived_3, arrived_1, arrived_2 = [travel(panel[i], every) for i in (3, 1, 2)]
    arrived_0 = travel(leading_piece, nearest)
    carried = [x[:NB] for x in arrived_0]
    carried = carried + travel(carried[-1], range(middle, n_pairs - 1))[1:]
    high = swap_rows(chosen(arrived_2, arrived_3), 2)
    high, across, blocks, *rest = together(
        high, across, blocks, *arrived_3, *arrived_1, *arrived_2, *arrived_0, *carried
    )
    arrived_3, rest = rest[:n_pairs], rest[n_pairs:]
    arrived_1, rest = rest[:n_pairs], rest[n_pairs:]
    arrived_2, rest = rest[:n_pairs], rest[n_pairs:]
    arrived_0, carried = rest[:middle], rest[middle:]

    masked_0 = [jnp.where(trailing, x, 0.0) for x in arrived_0]
    low = chosen(masked_0, arrived_1)
    held = jnp.where(near, low, high)
    held = [held] + [swap_rows(held, d) for d in range(1, n_rows)]
    carried.append(hop(carried[-1], n_pairs - 1))
    columns = jax.ShapeDtypeStruct((local_rows, 2 * NB), jnp.bfloat16)
    half_columns = jax.ShapeDtypeStruct((local_rows // 2, 2 * NB), jnp.bfloat16)
    masked = call(
        functools.partial(mask_kernel, n_rows, n_cols),
        "masked",
        (columns, columns, half_columns, half_columns),
        ids,
        adjoint,
        swap(after(adjoint, high)),
    )
    pieces = here(masked_0), here(arrived_1), here(arrived_2), here(arrived_3)
    turned, low, *block_sums = call(
        functools.partial(column_kernel, n_rows),
        "columns",
        (
            jax.ShapeDtypeStruct((NB, local_rows), jnp.float32),
            jax.ShapeDtypeStruct((NB, 2 * NB), jnp.float32),
        )
        + (SQUARE,) * n_rows,
        ids,
        *masked,
        *pieces,
        scratch=(pltpu.VMEM((4, NB, NB), jnp.float32),),
    )

    rest = together(*held, turned, low, *block_sums, *carried)
    held, (turned, low), rest = rest[:n_rows], rest[n_rows : n_rows + 2], rest[n_rows + 2 :]
    block_sums, carried = rest[:n_rows], here(rest[n_rows:])
    turned_other, blocks_other, across_other = swap(turned), swap(blocks), swap(across)

    height = 2 * NB // n_rows
    *shares, product = call(
        functools.partial(row_kernel, n_pairs),
        "rows",
        (SQUARE,) * n_pairs + (jax.ShapeDtypeStruct((local_rows, NB), jnp.float32),),
        ids,
        *masked,
        *held,
        adjoint,
        scratch=(pltpu.VMEM((n_pairs, NB, NB), jnp.float32),),
    )
    slices = call(
        functools.partial(sum_kernel, n_rows),
        "sums",
        (jax.ShapeDtypeStruct((height, NB), jnp.float32),) * n_rows,
        ids,
        turned,
        turned_other,
        product,
        low,
        scratch=(pltpu.VMEM((n_rows, height, NB), jnp.float32),),
    )
    rest = together(blocks_other, across_other, carried, *slices, *shares, *block_sums)
    (blocks_other, across_other, carried), rest = rest[:3], rest[3:]
    slices, shares, block_sums = (
        rest[:n_rows],
        rest[n_rows : n_rows + n_pairs],
        rest[n_rows + n_pairs :],
    )

    def folded(values, bit):
        kept = {d: value for d, value in values.items() if not d & bit}
        moved = {d: swap_pairs(value, bit) for d, value in values.items() if d & bit}
        return kept, moved

    def added(kept, moved, bit):
        return {d: value + moved[d ^ bit] for d, value in kept.items()}

    nearest_share, shares = shares[1], {d: x for d, x in enumerate(shares) if d != 1}
    kept, moved = folded(shares, 1)
    slices = [slices[0]] + [swap_rows(slices[d], d) for d in range(1, n_rows)]
    carried = jnp.where(row_id < 2, carried, swap_rows(carried, 2))
    rest = together(
        carried, nearest_share, *block_sums, *slices, *kept.values(), *moved.values()
    )
    (carried, nearest_share), rest = rest[:2], rest[2:]
    block_sums, rest = rest[:n_rows], rest[n_rows:]
    total, rest = sum(rest[1:n_rows], rest[0]), rest[n_rows:]
    kept, moved = dict(zip(kept, rest)), dict(zip(moved, rest[len(kept) :]))
    own_share = kept.pop(0)
    shares = added(kept, moved, 1)
    bit = 2
    while bit < n_pairs // 2:
        shares[0] = jnp.zeros_like(own_share)
        shares = added(*folded(shares, bit), bit)
        own_share = own_share + shares.pop(0)
        bit *= 2
    moved = swap_pairs(shares[bit], bit)
    total_other = swap_pairs(total, 1)
    block_sums = [block_sums[0]] + [swap_rows(block_sums[d], d) for d in range(1, n_rows)]
    rest = together(own_share, moved, nearest_share, carried, total, total_other, *block_sums)
    own_share, moved, nearest_share, carried, total, total_other = rest[:6]
    total, owned = total + total_other, sum(rest[7:], rest[6])

    def owner(r, p, k):
        half = 0 if r // 2 == p % 2 else 1
        return p % 2 * 2 + r % 2, p // 2 + half * (n_pairs // 2), k

    owned = send(owned, owner)
    bit = 2
    while bit < n_pairs:
        total = total + swap_pairs(total, bit)
        bit *= 2
    carried = [carried, swap_rows(carried, 1)]
    nearest_share = swap_pairs(nearest_share, 1)
    owned, total, nearest_share, *carried = together(owned, total, nearest_share, *carried)
    shares = own_share, moved, nearest_share

    mine, solved = call(
        functools.partial(solve_kernel, 3), "solve", (SQUARE, SQUARE), ids, *shares, owned, *carried
    )
    sums = [total] + [swap_rows(total, d) for d in range(1, n_rows)]
    second, *rest = together(swap(solved), *[swap(x) for x in carried], *sums)
    carried_other, sums = rest[:2], jnp.concatenate(rest[2:], 0)
    sums_other = swap(sums)
    lead = call(
        lead_kernel,
        "lead",
        SQUARE,
        ids,
        *carried,
        *carried_other,
        blocks,
        across,
        blocks_other,
        across_other,
        sums,
        sums_other,
    )
    result = call(end_kernel, "end", SQUARE, ids, mine, solved, second, *carried, lead)
    results, others, bit = {0: result}, {}, n_pairs // 2
    while bit:
        for d, value in list(results.items()):
            results[d ^ bit] = swap_pairs(value, bit)
        if bit == 2:
            results[1] = swap_pairs(result, 1)
            others[0] = swap(result)
            names = sorted(results)
            rest = together(others[0], *[results[d] for d in names])
            others[0], results = rest[0], dict(zip(names, rest[1:]))
            for d in names:
                if d ^ 1 not in results:
                    results[d ^ 1] = swap_pairs(results[d], 1)
            break
        bit //= 2
    for d in range(n_pairs):
        if d not in others:
            others[d] = swap(results[d])
    return call(
        functools.partial(place_kernel, n_pairs),
        "place",
        jax.ShapeDtypeStruct((local_rows, 2 * NB), jnp.float32),
        ids,
        *[results[d] for d in range(n_pairs)],
        *[others[d] for d in range(n_pairs)],
    )


def solution(mesh):
    placed = (P("row", "col"), P("row", "col"))
    return jax.shard_map(
        local, mesh=mesh, in_specs=placed, out_specs=P("row", None), check_vma=False
    )
```

```python
import functools

import jax
import jax.numpy as jnp
from jax import lax
from jax.experimental import pallas as pl
from jax.experimental.pallas import tpu as pltpu
from jax.sharding import PartitionSpec as P

NB = 256
ROW, PAIR, LANE = 0, 1, 2
SQUARE = jax.ShapeDtypeStruct((NB, NB), jnp.float32)


def dot(left, right):
    return jnp.dot(
        left, right, precision=lax.Precision.HIGHEST, preferred_element_type=jnp.float32
    )


def split(value):
    high = value.astype(jnp.bfloat16)
    return high, (value - high.astype(jnp.float32)).astype(jnp.bfloat16)


def dot3(left, right):
    once = functools.partial(jnp.dot, preferred_element_type=jnp.float32)
    return once(left[0], right[0]) + (once(left[0], right[1]) + once(left[1], right[0]))


def quick(left, right):
    return dot3(split(left), split(right))


def positions():
    rows = lax.broadcasted_iota(jnp.int32, (NB, NB), 0)
    cols = lax.broadcasted_iota(jnp.int32, (NB, NB), 1)
    return rows, cols


def call(kernel, name, out_shape, ids, *arrays, scratch=()):
    sizes = [x.size * x.dtype.itemsize for x in (*arrays, *jax.tree.leaves(out_shape))]
    return pl.pallas_call(
        kernel,
        out_shape=out_shape,
        in_specs=[pl.BlockSpec(memory_space=pltpu.SMEM)]
        + [pl.BlockSpec(memory_space=pltpu.VMEM)] * len(arrays),
        scratch_shapes=list(scratch),
        name=name,
        cost_estimate=pl.CostEstimate(flops=1, bytes_accessed=1, transcendentals=0),
        compiler_params=pltpu.CompilerParams(vmem_limit_bytes=min(60, 16 + sum(sizes) // 2**19) * 2**20),
    )(ids, *arrays)


def inverse_kernel(ids, block_ref, out_ref):
    @pl.when((ids[PAIR] == 0) & (ids[ROW] < 2))
    def _():
        half = NB // 2
        rows = lax.broadcasted_iota(jnp.int32, (half, half), 0)
        cols = lax.broadcasted_iota(jnp.int32, (half, half), 1)
        blocks = [block_ref[:half, :half], block_ref[half:, half:]]
        diagonal = rows == cols
        inverses = [
            jnp.where(diagonal, 1.0 / jnp.where(diagonal, x, 1.0), 0.0) for x in blocks
        ]
        size = 1
        while size < half:
            corner = (
                (rows // (2 * size) == cols // (2 * size))
                & (rows // size % 2 == 1)
                & (cols // size % 2 == 0)
            )
            inner = [dot(jnp.where(corner, x, 0.0), y) for x, y in zip(blocks, inverses)]
            inverses = [y - dot(y, x) for x, y in zip(inner, inverses)]
            size *= 2
        out_ref[:half, :half] = inverses[0]
        out_ref[:half, half:] = jnp.zeros((half, half), jnp.float32)
        out_ref[half:, half:] = inverses[1]
        out_ref[half:, :half] = -dot(inverses[1], dot(block_ref[half:, :half], inverses[0]))

    @pl.when((ids[PAIR] != 0) | (ids[ROW] >= 2))
    def _():
        out_ref[...] = jnp.zeros_like(out_ref)


def mask_kernel(n_rows, n_cols, ids, own, other, low_1, low_2, high_1, high_2):
    rows, cols = positions()
    below = rows - cols
    first = ids[LANE] == 0
    blocks = own.shape[0] // NB

    def masked(index, half, core):
        at = pl.ds(pl.multiple_of(index * NB, NB), NB)
        columns = slice(half * NB, (half + 1) * NB)
        mine = first if core == 0 else jnp.logical_not(first)
        value = jnp.where(mine, own[at, columns], other[at, columns])
        row_block = index * n_rows + ids[ROW]
        col_block = 2 * ids[PAIR] + half * n_cols + core
        least = jnp.where(row_block > col_block, -NB, jnp.where(row_block == col_block, 0, NB))
        least = jnp.where(row_block >= 2, least, NB)
        return split(jnp.where(below >= least, value, 0.0))

    @pl.loop(0, blocks)
    def _(index):
        for core in range(2):
            columns = slice(core * NB, (core + 1) * NB)
            at = pl.ds(pl.multiple_of(index * NB, NB), NB)
            low_1[at, columns], low_2[at, columns] = masked(index, 0, core)

    @pl.loop(0, blocks // 2)
    def _(index):
        for core in range(2):
            columns = slice(core * NB, (core + 1) * NB)
            at = pl.ds(pl.multiple_of(index * NB, NB), NB)
            high_1[at, columns], high_2[at, columns] = masked(index + blocks // 2, 1, core)


def column_kernel(n_rows, ids, low_1, low_2, high_1, high_2, *refs):
    refs, turned, low_ref, targets, sums = refs[:-7], refs[-7], refs[-6], refs[-5:-1], refs[-1]
    blocks = low_1.shape[0] // NB
    per_piece = blocks // 4
    low = jnp.zeros((NB, 2 * NB), jnp.float32)
    high = jnp.zeros((NB, 2 * NB), jnp.float32)
    for index, piece in enumerate(refs):
        for inner in range(per_piece):
            block = index * per_piece + inner
            at = slice(inner * NB, (inner + 1) * NB)
            value = piece[at, :]
            if block == 0:
                value = jnp.where(ids[ROW] >= 2, value, 0.0)
            value = value.T
            turned[:, block * NB : (block + 1) * NB] = value
            value = split(value)
            at = slice(block * NB, (block + 1) * NB)
            low += dot3(value, (low_1[at, :], low_2[at, :]))
            if block >= blocks // 2:
                block -= blocks // 2
                at = slice(block * NB, (block + 1) * NB)
                high += dot3(value, (high_1[at, :], high_2[at, :]))
    low_ref[...] = low
    sums[0], sums[1], sums[2], sums[3] = low[:, :NB], low[:, NB:], high[:, :NB], high[:, NB:]
    for d in range(n_rows):
        target = ids[ROW] ^ d
        targets[d][...] = sums[jnp.where(target // 2 == ids[PAIR] % 2, 0, 2) + target % 2]


def row_kernel(n_pairs, ids, low_1, low_2, high_1, high_2, v0, v1, v2, v3, adjoint, *refs):
    shares, product_ref, remaining = refs[:n_pairs], refs[-2], refs[-1]
    pair, row = ids[PAIR], ids[ROW]
    x_is_0 = row % 2 == 0
    near = row // 2 == pair % 2

    def panel(same, across):
        return split(
            jnp.concatenate(
                [jnp.where(x_is_0, same, across), jnp.where(x_is_0, across, same)], 0
            )
        )

    v0, v1, v2, v3 = [ref[...] for ref in (v0, v1, v2, v3)]
    panel_low = panel(jnp.where(near, v0, v2), jnp.where(near, v1, v3))
    panel_high = panel(jnp.where(near, v2, v0), jnp.where(near, v3, v1))
    for block in range(n_pairs):
        at = slice(block * NB, (block + 1) * NB)
        product = dot3((low_1[at, :], low_2[at, :]), panel_low)
        if block >= n_pairs // 2:
            upper = slice((block - n_pairs // 2) * NB, (block - n_pairs // 2 + 1) * NB)
            product += dot3((high_1[upper, :], high_2[upper, :]), panel_high)
        remaining[block] = jnp.where(pair == 0, adjoint[at, :NB], 0.0) - product
        product_ref[at, :] = product
    for d in range(n_pairs):
        shares[d][...] = remaining[pair ^ d]


def sum_kernel(n_rows, ids, turned, turned_other, product_ref, low, *refs):
    slices, sums = refs[:-1], refs[-1]
    first, first_pair = ids[LANE] == 0, ids[PAIR] == 0
    own = jnp.zeros((NB, NB), jnp.float32)
    other = jnp.zeros((NB, NB), jnp.float32)
    for block in range(turned.shape[1] // NB):
        at = slice(block * NB, (block + 1) * NB)
        product = split(product_ref[at, :])
        own += dot3(split(turned[:, at]), product)
        other += dot3(split(turned_other[:, at]), product)
    own_term = jnp.where(first, low[:, :NB], low[:, NB:])
    own_term = jnp.where(first_pair, own_term, 0.0)
    cross_term = jnp.where(first_pair, low[:, NB:], 0.0)
    own_sum = (own_term - own).T - own
    other_sum = jnp.where(first, cross_term.T - other, -other.T)
    height = 2 * NB // n_rows
    for index in range(n_rows // 2):
        at = slice(index * height, (index + 1) * height)
        sums[index] = own_sum[at]
        sums[index + n_rows // 2] = other_sum[at]
    for d in range(n_rows):
        slices[d][...] = sums[ids[ROW] ^ d]


def carried_blocks(ids, refs):
    same, other = [ref[...] for ref in refs]
    even = ids[ROW] % 2 == 0
    link = jnp.where(even, other, same)
    return jnp.where(ids[LANE] == 0, jnp.where(even, same, other), link), link


def solve_kernel(n_pairs, ids, *refs):
    shares, owned, carried = refs[:n_pairs], refs[n_pairs], refs[n_pairs + 1 : -2]
    total_ref, solved = refs[-2:]
    total = shares[0][...]
    for ref in shares[1:]:
        total = total + ref[...]
    total = total - owned[...].T
    inverse, _ = carried_blocks(ids, carried)
    total_ref[...] = total
    solved[...] = quick(total, inverse)


def end_kernel(ids, total, solved, second, c0, c1, c0_other, c1_other, blocks, across, blocks_other, across_other, sums_ref, sums_other, out_ref):
    row, first = ids[ROW], ids[LANE] == 0
    own, other = (c0, c1), (c0_other, c1_other)
    leading = (ids[PAIR] == 0) & (row < 2)

    @pl.when(jnp.logical_not(leading))
    def _():
        inverse, link = carried_blocks(ids, own)
        whole = quick(total[...] - quick(second[...], link), inverse)
        out_ref[...] = jnp.where(first, whole, solved[...])

    @pl.when(leading)
    def _():
        rows, cols = positions()
        in_first_row = row == 0

        def tril(x):
            return jnp.where(rows >= cols, x, 0.0)

        def phi(x):
            return jnp.where(rows > cols, x, jnp.where(rows == cols, 0.5 * x, 0.0))

        def diagonal_adjoint(block, block_bar, inverse_t, inverse):
            inner = phi(quick(block.T, block_bar))
            s = quick(inverse_t, quick(inner, inverse))
            return phi(s + s.T)

        def by_lane(own, other):
            return jnp.where(first, own, other), jnp.where(first, other, own)

        def held(own, other):
            firsts, seconds = by_lane(own[...], other[...])
            return [x[i * NB : (i + 1) * NB] for x in (firsts, seconds) for i in range(2)]

        mine, theirs = held(blocks, blocks_other), held(across, across_other)
        l0, a00, _, _ = [jnp.where(in_first_row, a, b) for a, b in zip(mine, theirs)]
        link, a10, l1, a11 = [jnp.where(in_first_row, b, a) for a, b in zip(mine, theirs)]
        inv0, _ = by_lane(*[jnp.where(in_first_row, x[...], y[...]) for x, y in (own, other)])
        _, inv1 = by_lane(*[jnp.where(in_first_row, y[...], x[...]) for x, y in (own, other)])

        def ordered(ref):
            value = ref[...]
            height = value.shape[0] // 4
            parts = [value[i * height : (i + 1) * height] for i in range(4)]
            swapped = jnp.concatenate([parts[1], parts[0], parts[3], parts[2]], 0)
            return jnp.where(in_first_row, value, swapped)

        sums_0, sums_1 = by_lane(ordered(sums_ref), ordered(sums_other))
        z00, z11, z10 = sums_0[:NB], sums_1[:NB], sums_0[NB:] + sums_1[NB:]
        inv1_t, inv0_t = inv1.T, inv0.T
        cross = quick(inv1_t, z10)
        k1 = tril(a11 - quick(inv1_t, z11))
        e1 = diagonal_adjoint(tril(l1), k1, inv1_t, inv1)
        rest = a10 - quick(e1 + e1.T, link) - cross
        g0 = quick(rest, inv0)
        k0 = tril(a00 - quick(inv0_t, z00 - quick(link.T, cross) + quick(rest.T, link)))
        e0 = diagonal_adjoint(tril(l0), k0, inv0_t, inv0)
        out_ref[...] = jnp.where(
            in_first_row, jnp.where(first, e0, 0.0), jnp.where(first, g0, e1)
        )


def place_kernel(n_pairs, ids, *refs):
    own, other, out_ref = refs[:n_pairs], refs[n_pairs:-1], refs[-1]
    first = ids[LANE] == 0
    for d in range(n_pairs):
        at = pl.ds(pl.multiple_of((ids[PAIR] ^ d) * NB, NB), NB)
        mine, theirs = own[d][...], other[d][...]
        out_ref[at, :NB] = jnp.where(first, mine, theirs)
        out_ref[at, NB:] = jnp.where(first, theirs, mine)


def after(value, *earlier):
    return lax.optimization_barrier((value, *earlier))[0]


def together(*values):
    return lax.optimization_barrier(values)


def local(factor, adjoint):
    n_rows = lax.axis_size("row")
    n_cols = lax.axis_size("col")
    n_pairs = n_cols // 2
    row_id = lax.axis_index("row")
    col_id = lax.axis_index("col")
    pair = col_id // 2
    lane = col_id % 2
    ids = jnp.stack([row_id, pair, lane])
    near = row_id // 2 == pair % 2
    first_pair = pair == 0
    local_rows = factor.shape[0]
    piece_rows = local_rows // 4

    def send(value, targets):
        edges = []
        for r in range(n_rows):
            for c in range(n_cols):
                target = targets(r, c // 2, c % 2)
                if target is not None:
                    edges.append((r * n_cols + c, target[0] * n_cols + target[1] * 2 + target[2]))
        return lax.ppermute(value, ("row", "col"), edges)

    def swap(value):
        return send(value, lambda r, p, k: (r, p, 1 - k))

    def swap_rows(value, d):
        return send(value, lambda r, p, k: (r ^ d, p, k))

    def swap_pairs(value, d):
        return send(value, lambda r, p, k: (r, p ^ d, k))

    panel = together(
        *[factor[i * piece_rows : (i + 1) * piece_rows, :NB] for i in range(4)], factor[:NB, :NB]
    )
    corner = panel[-1]

    def hop(value, number):
        return send(value, lambda r, p, k: (r, number, k) if p == number - 1 else None)

    def travel(value, hops):
        arrived = [value]
        for number in hops:
            arrived.append(hop(arrived[-1], number))
        return arrived

    def here(arrived):
        value = arrived[0]
        for p in range(1, len(arrived)):
            value = jnp.where(pair == p, arrived[p], value)
        return value

    middle = n_pairs // 2
    row_ids = jnp.arange(piece_rows, dtype=jnp.int32)
    trailing = ((row_ids >= NB) | (row_id >= 2))[:, None]

    def chosen(nearer, farther):
        start = pair // 2 % (piece_rows // NB) * NB
        value = here(nearer[:middle] + farther[middle:])
        return lax.dynamic_slice_in_dim(value, start, NB, 0)

    own_inverse = call(inverse_kernel, "inverse", SQUARE, ids, corner)
    carried = jnp.where((row_id == 1) & (lane == 0), corner, own_inverse)
    leading_piece = jnp.where(
        row_id < 2, jnp.concatenate([carried, panel[0][NB:]], 0), panel[0]
    )
    blocks = jnp.concatenate([corner, adjoint[:NB, :NB]], 0)
    across = send(blocks, lambda r, p, k: (r ^ 1, p, k) if p == 0 and r < 2 else None)
    every, nearest = range(1, n_pairs), range(1, middle)
    arrived_3, arrived_1, arrived_2 = [travel(panel[i], every) for i in (3, 1, 2)]
    arrived_0 = travel(leading_piece, nearest)
    carried = [x[:NB] for x in arrived_0]
    carried = carried + travel(carried[-1], range(middle, n_pairs - 1))[1:]
    high = swap_rows(chosen(arrived_2, arrived_3), 2)
    high, across, blocks, *rest = together(
        high, across, blocks, *arrived_3, *arrived_1, *arrived_2, *arrived_0, *carried
    )
    arrived_3, rest = rest[:n_pairs], rest[n_pairs:]
    arrived_1, rest = rest[:n_pairs], rest[n_pairs:]
    arrived_2, rest = rest[:n_pairs], rest[n_pairs:]
    arrived_0, carried = rest[:middle], rest[middle:]

    masked_0 = [jnp.where(trailing, x, 0.0) for x in arrived_0]
    low = chosen(masked_0, arrived_1)
    held = jnp.where(near, low, high)
    held = [held] + [swap_rows(held, d) for d in range(1, n_rows)]
    carried.append(hop(carried[-1], n_pairs - 1))
    columns = jax.ShapeDtypeStruct((local_rows, 2 * NB), jnp.bfloat16)
    half_columns = jax.ShapeDtypeStruct((local_rows // 2, 2 * NB), jnp.bfloat16)
    masked = call(
        functools.partial(mask_kernel, n_rows, n_cols),
        "masked",
        (columns, columns, half_columns, half_columns),
        ids,
        adjoint,
        swap(after(adjoint, high)),
    )
    pieces = here(masked_0), here(arrived_1), here(arrived_2), here(arrived_3)
    turned, low, *block_sums = call(
        functools.partial(column_kernel, n_rows),
        "columns",
        (
            jax.ShapeDtypeStruct((NB, local_rows), jnp.float32),
            jax.ShapeDtypeStruct((NB, 2 * NB), jnp.float32),
        )
        + (SQUARE,) * n_rows,
        ids,
        *masked,
        *pieces,
        scratch=(pltpu.VMEM((4, NB, NB), jnp.float32),),
    )

    rest = together(*held, turned, low, *block_sums, *carried)
    held, (turned, low), rest = rest[:n_rows], rest[n_rows : n_rows + 2], rest[n_rows + 2 :]
    block_sums, carried = rest[:n_rows], here(rest[n_rows:])
    turned_other, blocks_other, across_other = swap(turned), swap(blocks), swap(across)

    height = 2 * NB // n_rows
    *shares, product = call(
        functools.partial(row_kernel, n_pairs),
        "rows",
        (SQUARE,) * n_pairs + (jax.ShapeDtypeStruct((local_rows, NB), jnp.float32),),
        ids,
        *masked,
        *held,
        adjoint,
        scratch=(pltpu.VMEM((n_pairs, NB, NB), jnp.float32),),
    )
    slices = call(
        functools.partial(sum_kernel, n_rows),
        "sums",
        (jax.ShapeDtypeStruct((height, NB), jnp.float32),) * n_rows,
        ids,
        turned,
        turned_other,
        product,
        low,
        scratch=(pltpu.VMEM((n_rows, height, NB), jnp.float32),),
    )
    rest = together(blocks_other, across_other, carried, *slices, *shares, *block_sums)
    (blocks_other, across_other, carried), rest = rest[:3], rest[3:]
    slices, shares, block_sums = (
        rest[:n_rows],
        rest[n_rows : n_rows + n_pairs],
        rest[n_rows + n_pairs :],
    )

    def folded(values, bit):
        kept = {d: value for d, value in values.items() if not d & bit}
        moved = {d: swap_pairs(value, bit) for d, value in values.items() if d & bit}
        return kept, moved

    def added(kept, moved, bit):
        return {d: value + moved[d ^ bit] for d, value in kept.items()}

    nearest_share, shares = shares[1], {d: x for d, x in enumerate(shares) if d != 1}
    kept, moved = folded(shares, 1)
    slices = [slices[0]] + [swap_rows(slices[d], d) for d in range(1, n_rows)]
    carried = jnp.where(row_id < 2, carried, swap_rows(carried, 2))
    rest = together(
        carried, nearest_share, *block_sums, *slices, *kept.values(), *moved.values()
    )
    (carried, nearest_share), rest = rest[:2], rest[2:]
    block_sums, rest = rest[:n_rows], rest[n_rows:]
    total, rest = sum(rest[1:n_rows], rest[0]), rest[n_rows:]
    kept, moved = dict(zip(kept, rest)), dict(zip(moved, rest[len(kept) :]))
    own_share = kept.pop(0)
    shares = added(kept, moved, 1)
    bit = 2
    while bit < n_pairs // 2:
        shares[0] = jnp.zeros_like(own_share)
        shares = added(*folded(shares, bit), bit)
        own_share = own_share + shares.pop(0)
        bit *= 2
    moved = swap_pairs(shares[bit], bit)
    bit = 1
    while bit < n_pairs // 2:
        total = total + swap_pairs(total, bit)
        bit *= 2
    total_other = swap_pairs(total, bit)
    block_sums = [block_sums[0]] + [swap_rows(block_sums[d], d) for d in range(1, n_rows)]
    rest = together(own_share, moved, nearest_share, carried, total, total_other, *block_sums)
    own_share, moved, nearest_share, carried, total, total_other = rest[:6]
    total, owned = total + total_other, sum(rest[7:], rest[6])

    def owner(r, p, k):
        half = 0 if r // 2 == p % 2 else 1
        return p % 2 * 2 + r % 2, p // 2 + half * (n_pairs // 2), k

    owned = send(owned, owner)
    carried = [carried, swap_rows(carried, 1)]
    nearest_share = swap_pairs(nearest_share, 1)
    sums = [total] + [swap_rows(total, d) for d in range(1, n_rows)]
    owned, nearest_share, *rest = together(owned, nearest_share, *carried, *sums)
    carried, sums = rest[:2], jnp.concatenate(rest[2:], 0)
    shares = own_share, moved, nearest_share

    mine, solved = call(
        functools.partial(solve_kernel, 3), "solve", (SQUARE, SQUARE), ids, *shares, owned, *carried
    )
    second, sums_other = swap(solved), swap(sums)
    carried_other = [swap(x) for x in carried]
    result = call(
        end_kernel,
        "end",
        SQUARE,
        ids,
        mine,
        solved,
        second,
        *carried,
        *carried_other,
        blocks,
        across,
        blocks_other,
        across_other,
        sums,
        sums_other,
    )
    results, others, bit = {0: result}, {}, n_pairs // 2
    while bit:
        for d, value in list(results.items()):
            results[d ^ bit] = swap_pairs(value, bit)
        if bit == 2:
            results[1] = swap_pairs(result, 1)
            others[0] = swap(result)
            names = sorted(results)
            rest = together(others[0], *[results[d] for d in names])
            others[0], results = rest[0], dict(zip(names, rest[1:]))
            for d in names:
                if d ^ 1 not in results:
                    results[d ^ 1] = swap_pairs(results[d], 1)
            break
        bit //= 2
    for d in range(n_pairs):
        if d not in others:
            others[d] = swap(results[d])
    return call(
        functools.partial(place_kernel, n_pairs),
        "place",
        jax.ShapeDtypeStruct((local_rows, 2 * NB), jnp.float32),
        ids,
        *[results[d] for d in range(n_pairs)],
        *[others[d] for d in range(n_pairs)],
    )


def solution(mesh):
    placed = (P("row", "col"), P("row", "col"))
    return jax.shard_map(
        local, mesh=mesh, in_specs=placed, out_specs=P("row", None), check_vma=False
    )
```

```python
import functools

import jax
import jax.numpy as jnp
from jax import lax
from jax.experimental import pallas as pl
from jax.experimental.pallas import tpu as pltpu
from jax.sharding import PartitionSpec as P

NB = 256
ROW, PAIR, LANE = 0, 1, 2
SQUARE = jax.ShapeDtypeStruct((NB, NB), jnp.float32)


def dot(left, right):
    return jnp.dot(
        left, right, precision=lax.Precision.HIGHEST, preferred_element_type=jnp.float32
    )


def split(value):
    high = value.astype(jnp.bfloat16)
    return high, (value - high.astype(jnp.float32)).astype(jnp.bfloat16)


def dot3(left, right):
    once = functools.partial(jnp.dot, preferred_element_type=jnp.float32)
    return once(left[0], right[0]) + (once(left[0], right[1]) + once(left[1], right[0]))


def quick(left, right):
    return dot3(split(left), split(right))


def positions():
    rows = lax.broadcasted_iota(jnp.int32, (NB, NB), 0)
    cols = lax.broadcasted_iota(jnp.int32, (NB, NB), 1)
    return rows, cols


def call(kernel, name, out_shape, ids, *arrays, scratch=()):
    sizes = [x.size * x.dtype.itemsize for x in (*arrays, *jax.tree.leaves(out_shape))]
    return pl.pallas_call(
        kernel,
        out_shape=out_shape,
        in_specs=[pl.BlockSpec(memory_space=pltpu.SMEM)]
        + [pl.BlockSpec(memory_space=pltpu.VMEM)] * len(arrays),
        scratch_shapes=list(scratch),
        name=name,
        cost_estimate=pl.CostEstimate(flops=1, bytes_accessed=1, transcendentals=0),
        compiler_params=pltpu.CompilerParams(vmem_limit_bytes=min(60, 16 + sum(sizes) // 2**19) * 2**20),
    )(ids, *arrays)


def inverse_kernel(ids, block_ref, out_ref):
    @pl.when((ids[PAIR] == 0) & (ids[ROW] < 2))
    def _():
        half = NB // 2
        rows = lax.broadcasted_iota(jnp.int32, (half, half), 0)
        cols = lax.broadcasted_iota(jnp.int32, (half, half), 1)
        blocks = [block_ref[:half, :half], block_ref[half:, half:]]
        diagonal = rows == cols
        inverses = [
            jnp.where(diagonal, 1.0 / jnp.where(diagonal, x, 1.0), 0.0) for x in blocks
        ]
        size = 1
        while size < half:
            corner = (
                (rows // (2 * size) == cols // (2 * size))
                & (rows // size % 2 == 1)
                & (cols // size % 2 == 0)
            )
            inner = [dot(jnp.where(corner, x, 0.0), y) for x, y in zip(blocks, inverses)]
            inverses = [y - dot(y, x) for x, y in zip(inner, inverses)]
            size *= 2
        out_ref[:half, :half] = inverses[0]
        out_ref[:half, half:] = jnp.zeros((half, half), jnp.float32)
        out_ref[half:, half:] = inverses[1]
        out_ref[half:, :half] = -dot(inverses[1], dot(block_ref[half:, :half], inverses[0]))

    @pl.when((ids[PAIR] != 0) | (ids[ROW] >= 2))
    def _():
        out_ref[...] = jnp.zeros_like(out_ref)


def mask_kernel(n_rows, n_cols, ids, own, other, low_1, low_2, high_1, high_2):
    rows, cols = positions()
    below = rows - cols
    first = ids[LANE] == 0
    blocks = own.shape[0] // NB

    def masked(index, half, core):
        at = pl.ds(pl.multiple_of(index * NB, NB), NB)
        columns = slice(half * NB, (half + 1) * NB)
        mine = first if core == 0 else jnp.logical_not(first)
        value = jnp.where(mine, own[at, columns], other[at, columns])
        row_block = index * n_rows + ids[ROW]
        col_block = 2 * ids[PAIR] + half * n_cols + core
        least = jnp.where(row_block > col_block, -NB, jnp.where(row_block == col_block, 0, NB))
        least = jnp.where(row_block >= 2, least, NB)
        return split(jnp.where(below >= least, value, 0.0))

    @pl.loop(0, blocks)
    def _(index):
        for core in range(2):
            columns = slice(core * NB, (core + 1) * NB)
            at = pl.ds(pl.multiple_of(index * NB, NB), NB)
            low_1[at, columns], low_2[at, columns] = masked(index, 0, core)

    @pl.loop(0, blocks // 2)
    def _(index):
        for core in range(2):
            columns = slice(core * NB, (core + 1) * NB)
            at = pl.ds(pl.multiple_of(index * NB, NB), NB)
            high_1[at, columns], high_2[at, columns] = masked(index + blocks // 2, 1, core)


def column_kernel(n_rows, ids, low_1, low_2, high_1, high_2, *refs):
    refs, turned, low_ref, targets, sums = refs[:-7], refs[-7], refs[-6], refs[-5:-1], refs[-1]
    blocks = low_1.shape[0] // NB
    per_piece = blocks // 4
    low = jnp.zeros((NB, 2 * NB), jnp.float32)
    high = jnp.zeros((NB, 2 * NB), jnp.float32)
    for index, piece in enumerate(refs):
        for inner in range(per_piece):
            block = index * per_piece + inner
            at = slice(inner * NB, (inner + 1) * NB)
            value = piece[at, :]
            if block == 0:
                value = jnp.where(ids[ROW] >= 2, value, 0.0)
            value = value.T
            turned[:, block * NB : (block + 1) * NB] = value
            value = split(value)
            at = slice(block * NB, (block + 1) * NB)
            low += dot3(value, (low_1[at, :], low_2[at, :]))
            if block >= blocks // 2:
                block -= blocks // 2
                at = slice(block * NB, (block + 1) * NB)
                high += dot3(value, (high_1[at, :], high_2[at, :]))
    low_ref[...] = low
    sums[0], sums[1], sums[2], sums[3] = low[:, :NB], low[:, NB:], high[:, :NB], high[:, NB:]
    for d in range(n_rows):
        target = ids[ROW] ^ d
        targets[d][...] = sums[jnp.where(target // 2 == ids[PAIR] % 2, 0, 2) + target % 2]


def row_kernel(n_pairs, ids, low_1, low_2, high_1, high_2, v0, v1, v2, v3, adjoint, *refs):
    arrived, refs = refs[:n_pairs], refs[n_pairs:]
    evens, (odds, product_ref, carried, remaining) = refs[:-4], refs[-4:]
    pair, row = ids[PAIR], ids[ROW]
    x_is_0 = row % 2 == 0
    near = row // 2 == pair % 2

    def panel(same, across):
        return split(
            jnp.concatenate(
                [jnp.where(x_is_0, same, across), jnp.where(x_is_0, across, same)], 0
            )
        )

    v0, v1, v2, v3 = [ref[...] for ref in (v0, v1, v2, v3)]
    panel_low = panel(jnp.where(near, v0, v2), jnp.where(near, v1, v3))
    panel_high = panel(jnp.where(near, v2, v0), jnp.where(near, v3, v1))
    for block in range(n_pairs):
        at = slice(block * NB, (block + 1) * NB)
        product = dot3((low_1[at, :], low_2[at, :]), panel_low)
        if block >= n_pairs // 2:
            upper = slice((block - n_pairs // 2) * NB, (block - n_pairs // 2 + 1) * NB)
            product += dot3((high_1[upper, :], high_2[upper, :]), panel_high)
        remaining[block] = jnp.where(pair == 0, adjoint[at, :NB], 0.0) - product
        product_ref[at, :] = product
    for d in range(0, n_pairs, 2):
        evens[d // 2][...] = remaining[pair ^ d]
        odds[d // 2 * NB : (d // 2 + 1) * NB, :] = remaining[pair ^ (d + 1)]
    value = arrived[0][...]
    for p in range(1, n_pairs):
        value = jnp.where(pair == p, arrived[p][...], value)
    carried[...] = value


def sum_kernel(n_rows, ids, turned, turned_other, product_ref, low, *refs):
    slices, sums = refs[:-1], refs[-1]
    first, first_pair = ids[LANE] == 0, ids[PAIR] == 0
    own = jnp.zeros((NB, NB), jnp.float32)
    other = jnp.zeros((NB, NB), jnp.float32)
    for block in range(turned.shape[1] // NB):
        at = slice(block * NB, (block + 1) * NB)
        product = split(product_ref[at, :])
        own += dot3(split(turned[:, at]), product)
        other += dot3(split(turned_other[:, at]), product)
    own_term = jnp.where(first, low[:, :NB], low[:, NB:])
    own_term = jnp.where(first_pair, own_term, 0.0)
    cross_term = jnp.where(first_pair, low[:, NB:], 0.0)
    own_sum = (own_term - own).T - own
    other_sum = jnp.where(first, cross_term.T - other, -other.T)
    height = 2 * NB // n_rows
    for index in range(n_rows // 2):
        at = slice(index * height, (index + 1) * height)
        sums[index] = own_sum[at]
        sums[index + n_rows // 2] = other_sum[at]
    for d in range(n_rows):
        slices[d][...] = sums[ids[ROW] ^ d]


def carried_blocks(ids, refs):
    same, other = [ref[...] for ref in refs]
    even = ids[ROW] % 2 == 0
    link = jnp.where(even, other, same)
    return jnp.where(ids[LANE] == 0, jnp.where(even, same, other), link), link


def solve_kernel(n_pairs, ids, *refs):
    shares, owned, carried = refs[:n_pairs], refs[n_pairs], refs[n_pairs + 1 : -2]
    total_ref, solved = refs[-2:]
    total = shares[0][...]
    for ref in shares[1:]:
        total = total + ref[:NB, :]
    total = total - owned[...].T
    inverse, _ = carried_blocks(ids, carried)
    total_ref[...] = total
    solved[...] = quick(total, inverse)


def end_kernel(ids, total, solved, second, c0, c1, c0_other, c1_other, blocks, across, blocks_other, across_other, sums_ref, sums_other, out_ref):
    row, first = ids[ROW], ids[LANE] == 0
    own, other = (c0, c1), (c0_other, c1_other)
    leading = (ids[PAIR] == 0) & (row < 2)

    @pl.when(jnp.logical_not(leading))
    def _():
        inverse, link = carried_blocks(ids, own)
        whole = quick(total[...] - quick(second[...], link), inverse)
        out_ref[...] = jnp.where(first, whole, solved[...])

    @pl.when(leading)
    def _():
        rows, cols = positions()
        in_first_row = row == 0

        def tril(x):
            return jnp.where(rows >= cols, x, 0.0)

        def phi(x):
            return jnp.where(rows > cols, x, jnp.where(rows == cols, 0.5 * x, 0.0))

        def diagonal_adjoint(block, block_bar, inverse_t, inverse):
            inner = phi(quick(block.T, block_bar))
            s = quick(inverse_t, quick(inner, inverse))
            return phi(s + s.T)

        def by_lane(own, other):
            return jnp.where(first, own, other), jnp.where(first, other, own)

        def held(own, other):
            firsts, seconds = by_lane(own[...], other[...])
            return [x[i * NB : (i + 1) * NB] for x in (firsts, seconds) for i in range(2)]

        mine, theirs = held(blocks, blocks_other), held(across, across_other)
        l0, a00, _, _ = [jnp.where(in_first_row, a, b) for a, b in zip(mine, theirs)]
        link, a10, l1, a11 = [jnp.where(in_first_row, b, a) for a, b in zip(mine, theirs)]
        inv0, _ = by_lane(*[jnp.where(in_first_row, x[...], y[...]) for x, y in (own, other)])
        _, inv1 = by_lane(*[jnp.where(in_first_row, y[...], x[...]) for x, y in (own, other)])

        def ordered(ref):
            value = ref[...]
            height = value.shape[0] // 4
            parts = [value[i * height : (i + 1) * height] for i in range(4)]
            swapped = jnp.concatenate([parts[1], parts[0], parts[3], parts[2]], 0)
            return jnp.where(in_first_row, value, swapped)

        sums_0, sums_1 = by_lane(ordered(sums_ref), ordered(sums_other))
        z00, z11, z10 = sums_0[:NB], sums_1[:NB], sums_0[NB:] + sums_1[NB:]
        inv1_t, inv0_t = inv1.T, inv0.T
        cross = quick(inv1_t, z10)
        k1 = tril(a11 - quick(inv1_t, z11))
        e1 = diagonal_adjoint(tril(l1), k1, inv1_t, inv1)
        early = quick(a10 - cross, inv0)
        earlier = a00 - quick(inv0_t, z00 - quick(link.T, cross))
        g0 = early - quick(e1 + e1.T, quick(link, inv0))
        k0 = tril(earlier - quick(g0.T, link))
        e0 = diagonal_adjoint(tril(l0), k0, inv0_t, inv0)
        out_ref[...] = jnp.where(
            in_first_row, jnp.where(first, e0, 0.0), jnp.where(first, g0, e1)
        )


def place_kernel(n_pairs, ids, *refs):
    own, other, out_ref = refs[:n_pairs], refs[n_pairs:-1], refs[-1]
    first = ids[LANE] == 0
    for d in range(n_pairs):
        at = pl.ds(pl.multiple_of((ids[PAIR] ^ d) * NB, NB), NB)
        mine, theirs = own[d][...], other[d][...]
        out_ref[at, :NB] = jnp.where(first, mine, theirs)
        out_ref[at, NB:] = jnp.where(first, theirs, mine)


def after(value, *earlier):
    return lax.optimization_barrier((value, *earlier))[0]


def together(*values):
    return lax.optimization_barrier(values)


def local(factor, adjoint):
    n_rows = lax.axis_size("row")
    n_cols = lax.axis_size("col")
    n_pairs = n_cols // 2
    row_id = lax.axis_index("row")
    col_id = lax.axis_index("col")
    pair = col_id // 2
    lane = col_id % 2
    ids = jnp.stack([row_id, pair, lane])
    near = row_id // 2 == pair % 2
    first_pair = pair == 0
    local_rows = factor.shape[0]
    piece_rows = local_rows // 4

    def send(value, targets):
        edges = []
        for r in range(n_rows):
            for c in range(n_cols):
                target = targets(r, c // 2, c % 2)
                if target is not None:
                    edges.append((r * n_cols + c, target[0] * n_cols + target[1] * 2 + target[2]))
        return lax.ppermute(value, ("row", "col"), edges)

    def swap(value):
        return send(value, lambda r, p, k: (r, p, 1 - k))

    def swap_rows(value, d):
        return send(value, lambda r, p, k: (r ^ d, p, k))

    def swap_pairs(value, d):
        return send(value, lambda r, p, k: (r, p ^ d, k))

    panel = together(
        *[factor[i * piece_rows : (i + 1) * piece_rows, :NB] for i in range(4)], factor[:NB, :NB]
    )
    corner = panel[-1]

    def hop(value, number):
        return send(value, lambda r, p, k: (r, number, k) if p == number - 1 else None)

    def travel(value, hops):
        arrived = [value]
        for number in hops:
            arrived.append(hop(arrived[-1], number))
        return arrived

    def here(arrived):
        value = arrived[0]
        for p in range(1, len(arrived)):
            value = jnp.where(pair == p, arrived[p], value)
        return value

    middle = n_pairs // 2
    row_ids = jnp.arange(piece_rows, dtype=jnp.int32)
    trailing = ((row_ids >= NB) | (row_id >= 2))[:, None]

    def chosen(nearer, farther):
        start = pair // 2 % (piece_rows // NB) * NB
        value = here(nearer[:middle] + farther[middle:])
        return lax.dynamic_slice_in_dim(value, start, NB, 0)

    own_inverse = call(inverse_kernel, "inverse", SQUARE, ids, corner)
    carried = jnp.where((row_id == 1) & (lane == 0), corner, own_inverse)
    leading_piece = jnp.where(
        row_id < 2, jnp.concatenate([carried, panel[0][NB:]], 0), panel[0]
    )
    blocks = jnp.concatenate([corner, adjoint[:NB, :NB]], 0)
    across = send(blocks, lambda r, p, k: (r ^ 1, p, k) if p == 0 and r < 2 else None)
    every, nearest = range(1, n_pairs), range(1, middle)
    arrived_3, arrived_1, arrived_2 = [travel(panel[i], every) for i in (3, 1, 2)]
    arrived_0 = travel(leading_piece, nearest)
    carried = [x[:NB] for x in arrived_0]
    carried = carried + travel(carried[-1], range(middle, n_pairs - 1))[1:]
    high = swap_rows(chosen(arrived_2, arrived_3), 2)
    high, across, blocks, *rest = together(
        high, across, blocks, *arrived_3, *arrived_1, *arrived_2, *arrived_0, *carried
    )
    arrived_3, rest = rest[:n_pairs], rest[n_pairs:]
    arrived_1, rest = rest[:n_pairs], rest[n_pairs:]
    arrived_2, rest = rest[:n_pairs], rest[n_pairs:]
    arrived_0, carried = rest[:middle], rest[middle:]

    masked_0 = [jnp.where(trailing, x, 0.0) for x in arrived_0]
    low = chosen(masked_0, arrived_1)
    held = jnp.where(near, low, high)
    held = [held] + [swap_rows(held, d) for d in range(1, n_rows)]
    carried.append(hop(carried[-1], n_pairs - 1))
    columns = jax.ShapeDtypeStruct((local_rows, 2 * NB), jnp.bfloat16)
    half_columns = jax.ShapeDtypeStruct((local_rows // 2, 2 * NB), jnp.bfloat16)
    masked = call(
        functools.partial(mask_kernel, n_rows, n_cols),
        "masked",
        (columns, columns, half_columns, half_columns),
        ids,
        adjoint,
        swap(after(adjoint, high)),
    )
    pieces = here(masked_0), here(arrived_1), here(arrived_2), here(arrived_3)
    turned, low, *block_sums = call(
        functools.partial(column_kernel, n_rows),
        "columns",
        (
            jax.ShapeDtypeStruct((NB, local_rows), jnp.float32),
            jax.ShapeDtypeStruct((NB, 2 * NB), jnp.float32),
        )
        + (SQUARE,) * n_rows,
        ids,
        *masked,
        *pieces,
        scratch=(pltpu.VMEM((4, NB, NB), jnp.float32),),
    )

    rest = together(*held, turned, low, *block_sums, *carried)
    held, (turned, low), rest = rest[:n_rows], rest[n_rows : n_rows + 2], rest[n_rows + 2 :]
    block_sums, carried = rest[:n_rows], rest[n_rows:]
    turned_other, blocks_other, across_other = swap(turned), swap(blocks), swap(across)

    height = 2 * NB // n_rows
    *evens, odds, product, carried = call(
        functools.partial(row_kernel, n_pairs),
        "rows",
        (SQUARE,) * middle
        + (
            jax.ShapeDtypeStruct((middle * NB, NB), jnp.float32),
            jax.ShapeDtypeStruct((local_rows, NB), jnp.float32),
            SQUARE,
        ),
        ids,
        *masked,
        *held,
        adjoint,
        *carried,
        scratch=(pltpu.VMEM((n_pairs, NB, NB), jnp.float32),),
    )
    slices = call(
        functools.partial(sum_kernel, n_rows),
        "sums",
        (jax.ShapeDtypeStruct((height, NB), jnp.float32),) * n_rows,
        ids,
        turned,
        turned_other,
        product,
        low,
        scratch=(pltpu.VMEM((n_rows, height, NB), jnp.float32),),
    )
    rest = together(blocks_other, across_other, carried, odds, *slices, *evens, *block_sums)
    (blocks_other, across_other, carried, odds), rest = rest[:4], rest[4:]
    slices, evens, block_sums = (
        rest[:n_rows],
        rest[n_rows : n_rows + middle],
        rest[n_rows + middle :],
    )

    def folded(values, bit):
        kept = {d: value for d, value in values.items() if not d & bit}
        moved = {d: swap_pairs(value, bit) for d, value in values.items() if d & bit}
        return kept, moved

    def added(kept, moved, bit):
        return {d: value + moved[d ^ bit] for d, value in kept.items()}

    slices = [slices[0]] + [swap_rows(slices[d], d) for d in range(1, n_rows)]
    beyond = send(carried, lambda r, p, k: (r + 2, p, k) if r < 2 else None)
    carried = jnp.where(row_id < 2, carried, beyond)
    rest = together(carried, swap_pairs(odds, 1), *block_sums, *slices, *evens)
    (carried, odds), rest = rest[:2], rest[2:]
    block_sums, rest = rest[:n_rows], rest[n_rows:]
    total, evens = sum(rest[1:n_rows], rest[0]), rest[n_rows:]
    own_share = evens[0]
    shares = {
        2 * i: evens[i] + odds[i * NB : (i + 1) * NB] for i in range(1, middle)
    }
    bit = 2
    while bit < n_pairs // 2:
        shares[0] = jnp.zeros_like(own_share)
        shares = added(*folded(shares, bit), bit)
        own_share = own_share + shares.pop(0)
        bit *= 2
    moved = swap_pairs(shares[bit], bit)
    def toward_first(value, bit):
        return send(
            value, lambda r, p, k: (r, p - bit, k) if p & bit and not p & (bit - 1) else None
        )

    bit = 1
    while bit < n_pairs // 2:
        total = total + toward_first(total, bit)
        bit *= 2
    total_other = toward_first(total, bit)
    block_sums = [block_sums[0]] + [swap_rows(block_sums[d], d) for d in range(1, n_rows)]
    rest = together(own_share, moved, odds, carried, total, total_other, *block_sums)
    own_share, moved, odds, carried, total, total_other = rest[:6]
    total, owned = total + total_other, sum(rest[7:], rest[6])

    def owner(r, p, k):
        half = 0 if r // 2 == p % 2 else 1
        return p % 2 * 2 + r % 2, p // 2 + half * (n_pairs // 2), k

    owned = send(owned, owner)
    carried = [carried, swap_rows(carried, 1)]
    sums = [total] + [
        send(total, lambda r, p, k, d=d: (r ^ d, p, k) if p == 0 and r ^ d < 2 else None)
        for d in range(1, n_rows)
    ]
    owned, *rest = together(owned, *carried, *sums)
    carried, sums = rest[:2], jnp.concatenate(rest[2:], 0)
    shares = own_share, moved, odds

    mine, solved = call(
        functools.partial(solve_kernel, 3), "solve", (SQUARE, SQUARE), ids, *shares, owned, *carried
    )
    second, sums_other = swap(solved), swap(sums)
    carried_other = [swap(x) for x in carried]
    result = call(
        end_kernel,
        "end",
        SQUARE,
        ids,
        mine,
        solved,
        second,
        *carried,
        *carried_other,
        blocks,
        across,
        blocks_other,
        across_other,
        sums,
        sums_other,
    )
    results, others, bit = {0: result}, {}, n_pairs // 2
    while bit:
        for d, value in list(results.items()):
            results[d ^ bit] = swap_pairs(value, bit)
        if bit == 2:
            results[1] = swap_pairs(result, 1)
            others[0] = swap(result)
            names = sorted(results)
            rest = together(others[0], *[results[d] for d in names])
            others[0], results = rest[0], dict(zip(names, rest[1:]))
            for d in names:
                if d ^ 1 not in results:
                    results[d ^ 1] = swap_pairs(results[d], 1)
            break
        bit //= 2
    for d in range(n_pairs):
        if d not in others:
            others[d] = swap(results[d])
    return call(
        functools.partial(place_kernel, n_pairs),
        "place",
        jax.ShapeDtypeStruct((local_rows, 2 * NB), jnp.float32),
        ids,
        *[results[d] for d in range(n_pairs)],
        *[others[d] for d in range(n_pairs)],
    )


def solution(mesh):
    placed = (P("row", "col"), P("row", "col"))
    return jax.shard_map(
        local, mesh=mesh, in_specs=placed, out_specs=P("row", None), check_vma=False
    )
```

```python
import functools

import jax
import jax.numpy as jnp
from jax import lax
from jax.experimental import pallas as pl
from jax.experimental.pallas import tpu as pltpu
from jax.sharding import PartitionSpec as P

NB = 256
ROW, PAIR, LANE = 0, 1, 2
SQUARE = jax.ShapeDtypeStruct((NB, NB), jnp.float32)


def dot(left, right):
    return jnp.dot(
        left, right, precision=lax.Precision.HIGHEST, preferred_element_type=jnp.float32
    )


def split(value):
    high = value.astype(jnp.bfloat16)
    return high, (value - high.astype(jnp.float32)).astype(jnp.bfloat16)


def dot3(left, right):
    once = functools.partial(jnp.dot, preferred_element_type=jnp.float32)
    return once(left[0], right[0]) + (once(left[0], right[1]) + once(left[1], right[0]))


def quick(left, right):
    return dot3(split(left), split(right))


def positions():
    rows = lax.broadcasted_iota(jnp.int32, (NB, NB), 0)
    cols = lax.broadcasted_iota(jnp.int32, (NB, NB), 1)
    return rows, cols


def call(kernel, name, out_shape, ids, *arrays, scratch=()):
    sizes = [x.size * x.dtype.itemsize for x in (*arrays, *jax.tree.leaves(out_shape))]
    return pl.pallas_call(
        kernel,
        out_shape=out_shape,
        in_specs=[pl.BlockSpec(memory_space=pltpu.SMEM)]
        + [pl.BlockSpec(memory_space=pltpu.VMEM)] * len(arrays),
        scratch_shapes=list(scratch),
        name=name,
        cost_estimate=pl.CostEstimate(flops=1, bytes_accessed=1, transcendentals=0),
        compiler_params=pltpu.CompilerParams(vmem_limit_bytes=min(60, 16 + sum(sizes) // 2**19) * 2**20),
    )(ids, *arrays)


def inverse_kernel(ids, block_ref, out_ref):
    @pl.when((ids[PAIR] == 0) & (ids[ROW] < 2))
    def _():
        half = NB // 2
        rows = lax.broadcasted_iota(jnp.int32, (half, half), 0)
        cols = lax.broadcasted_iota(jnp.int32, (half, half), 1)
        blocks = [block_ref[:half, :half], block_ref[half:, half:]]
        diagonal = rows == cols
        inverses = [
            jnp.where(diagonal, 1.0 / jnp.where(diagonal, x, 1.0), 0.0) for x in blocks
        ]
        size = 1
        while size < half:
            corner = (
                (rows // (2 * size) == cols // (2 * size))
                & (rows // size % 2 == 1)
                & (cols // size % 2 == 0)
            )
            inner = [dot(jnp.where(corner, x, 0.0), y) for x, y in zip(blocks, inverses)]
            inverses = [y - dot(y, x) for x, y in zip(inner, inverses)]
            size *= 2
        out_ref[:half, :half] = inverses[0]
        out_ref[:half, half:] = jnp.zeros((half, half), jnp.float32)
        out_ref[half:, half:] = inverses[1]
        out_ref[half:, :half] = -dot(inverses[1], dot(block_ref[half:, :half], inverses[0]))

    @pl.when((ids[PAIR] != 0) | (ids[ROW] >= 2))
    def _():
        out_ref[...] = jnp.zeros_like(out_ref)


def mask_kernel(n_rows, n_cols, ids, own, other, low_1, low_2, high_1, high_2):
    rows, cols = positions()
    below = rows - cols
    first = ids[LANE] == 0
    blocks = own.shape[0] // NB

    def masked(index, half, core):
        at = pl.ds(pl.multiple_of(index * NB, NB), NB)
        columns = slice(half * NB, (half + 1) * NB)
        mine = first if core == 0 else jnp.logical_not(first)
        value = jnp.where(mine, own[at, columns], other[at, columns])
        row_block = index * n_rows + ids[ROW]
        col_block = 2 * ids[PAIR] + half * n_cols + core
        least = jnp.where(row_block > col_block, -NB, jnp.where(row_block == col_block, 0, NB))
        least = jnp.where(row_block >= 2, least, NB)
        return split(jnp.where(below >= least, value, 0.0))

    @pl.loop(0, blocks)
    def _(index):
        for core in range(2):
            columns = slice(core * NB, (core + 1) * NB)
            at = pl.ds(pl.multiple_of(index * NB, NB), NB)
            low_1[at, columns], low_2[at, columns] = masked(index, 0, core)

    @pl.loop(0, blocks // 2)
    def _(index):
        for core in range(2):
            columns = slice(core * NB, (core + 1) * NB)
            at = pl.ds(pl.multiple_of(index * NB, NB), NB)
            high_1[at, columns], high_2[at, columns] = masked(index + blocks // 2, 1, core)


def column_kernel(n_rows, ids, low_1, low_2, high_1, high_2, *refs):
    refs, turned, low_ref, targets, sums = refs[:-7], refs[-7], refs[-6], refs[-5:-1], refs[-1]
    blocks = low_1.shape[0] // NB
    per_piece = blocks // 4
    low = jnp.zeros((NB, 2 * NB), jnp.float32)
    high = jnp.zeros((NB, 2 * NB), jnp.float32)
    for index, piece in enumerate(refs):
        for inner in range(per_piece):
            block = index * per_piece + inner
            at = slice(inner * NB, (inner + 1) * NB)
            value = piece[at, :]
            if block == 0:
                value = jnp.where(ids[ROW] >= 2, value, 0.0)
            value = value.T
            turned[:, block * NB : (block + 1) * NB] = value
            value = split(value)
            at = slice(block * NB, (block + 1) * NB)
            low += dot3(value, (low_1[at, :], low_2[at, :]))
            if block >= blocks // 2:
                block -= blocks // 2
                at = slice(block * NB, (block + 1) * NB)
                high += dot3(value, (high_1[at, :], high_2[at, :]))
    low_ref[...] = low
    sums[0], sums[1], sums[2], sums[3] = low[:, :NB], low[:, NB:], high[:, :NB], high[:, NB:]
    for d in range(n_rows):
        target = ids[ROW] ^ d
        targets[d][...] = sums[jnp.where(target // 2 == ids[PAIR] % 2, 0, 2) + target % 2]


def row_kernel(n_pairs, ids, low_1, low_2, high_1, high_2, v0, v1, v2, v3, adjoint, *refs):
    arrived, refs = refs[:n_pairs], refs[n_pairs:]
    evens, (odds, product_ref, carried, remaining) = refs[:-4], refs[-4:]
    pair, row = ids[PAIR], ids[ROW]
    x_is_0 = row % 2 == 0
    near = row // 2 == pair % 2

    def panel(same, across):
        return split(
            jnp.concatenate(
                [jnp.where(x_is_0, same, across), jnp.where(x_is_0, across, same)], 0
            )
        )

    v0, v1, v2, v3 = [ref[...] for ref in (v0, v1, v2, v3)]
    panel_low = panel(jnp.where(near, v0, v2), jnp.where(near, v1, v3))
    panel_high = panel(jnp.where(near, v2, v0), jnp.where(near, v3, v1))
    for block in range(n_pairs):
        at = slice(block * NB, (block + 1) * NB)
        product = dot3((low_1[at, :], low_2[at, :]), panel_low)
        if block >= n_pairs // 2:
            upper = slice((block - n_pairs // 2) * NB, (block - n_pairs // 2 + 1) * NB)
            product += dot3((high_1[upper, :], high_2[upper, :]), panel_high)
        remaining[block] = jnp.where(pair == 0, adjoint[at, :NB], 0.0) - product
        product_ref[at, :] = product
    for d in range(0, n_pairs, 2):
        evens[d // 2][...] = remaining[pair ^ d]
        odds[d // 2 * NB : (d // 2 + 1) * NB, :] = remaining[pair ^ (d + 1)]
    value = arrived[0][...]
    for p in range(1, n_pairs):
        value = jnp.where(pair == p, arrived[p][...], value)
    carried[...] = value


def sum_kernel(n_rows, ids, turned, turned_other, product_ref, low, *refs):
    slices, sums = refs[:-1], refs[-1]
    first, first_pair = ids[LANE] == 0, ids[PAIR] == 0
    own = jnp.zeros((NB, NB), jnp.float32)
    other = jnp.zeros((NB, NB), jnp.float32)
    for block in range(turned.shape[1] // NB):
        at = slice(block * NB, (block + 1) * NB)
        product = split(product_ref[at, :])
        own += dot3(split(turned[:, at]), product)
        other += dot3(split(turned_other[:, at]), product)
    own_term = jnp.where(first, low[:, :NB], low[:, NB:])
    own_term = jnp.where(first_pair, own_term, 0.0)
    cross_term = jnp.where(first_pair, low[:, NB:], 0.0)
    own_sum = (own_term - own).T - own
    other_sum = jnp.where(first, cross_term.T - other, -other.T)
    height = 2 * NB // n_rows
    for index in range(n_rows // 2):
        at = slice(index * height, (index + 1) * height)
        sums[index] = own_sum[at]
        sums[index + n_rows // 2] = other_sum[at]
    for d in range(n_rows):
        slices[d][...] = sums[ids[ROW] ^ d]


def carried_blocks(ids, refs):
    same, other = [ref[...] for ref in refs]
    even = ids[ROW] % 2 == 0
    link = jnp.where(even, other, same)
    return jnp.where(ids[LANE] == 0, jnp.where(even, same, other), link), link


def solve_kernel(n_pairs, ids, *refs):
    shares, owned, carried = refs[:n_pairs], refs[n_pairs], refs[n_pairs + 1 : -2]
    total_ref, solved = refs[-2:]
    total = shares[0][...]
    for ref in shares[1:]:
        total = total + ref[:NB, :]
    total = total - owned[...].T
    inverse, _ = carried_blocks(ids, carried)
    total_ref[...] = total
    solved[...] = quick(total, inverse)


def end_kernel(ids, total, solved, second, c0, c1, c0_other, c1_other, blocks, across, blocks_other, across_other, sums_ref, sums_other, out_ref):
    row, first = ids[ROW], ids[LANE] == 0
    own, other = (c0, c1), (c0_other, c1_other)
    leading = (ids[PAIR] == 0) & (row < 2)

    @pl.when(jnp.logical_not(leading))
    def _():
        inverse, link = carried_blocks(ids, own)
        whole = quick(total[...] - quick(second[...], link), inverse)
        out_ref[...] = jnp.where(first, whole, solved[...])

    @pl.when(leading)
    def _():
        rows, cols = positions()
        in_first_row = row == 0

        def tril(x):
            return jnp.where(rows >= cols, x, 0.0)

        def phi(x):
            return jnp.where(rows > cols, x, jnp.where(rows == cols, 0.5 * x, 0.0))

        def diagonal_adjoint(block, block_bar, inverse_t, inverse):
            inner = phi(quick(block.T, block_bar))
            s = quick(inverse_t, quick(inner, inverse))
            return phi(s + s.T)

        def by_lane(own, other):
            return jnp.where(first, own, other), jnp.where(first, other, own)

        def held(own, other):
            firsts, seconds = by_lane(own[...], other[...])
            return [x[i * NB : (i + 1) * NB] for x in (firsts, seconds) for i in range(2)]

        mine, theirs = held(blocks, blocks_other), held(across, across_other)
        l0, a00, _, _ = [jnp.where(in_first_row, a, b) for a, b in zip(mine, theirs)]
        link, a10, l1, a11 = [jnp.where(in_first_row, b, a) for a, b in zip(mine, theirs)]
        inv0, _ = by_lane(*[jnp.where(in_first_row, x[...], y[...]) for x, y in (own, other)])
        _, inv1 = by_lane(*[jnp.where(in_first_row, y[...], x[...]) for x, y in (own, other)])

        def ordered(ref):
            value = ref[...]
            height = value.shape[0] // 4
            parts = [value[i * height : (i + 1) * height] for i in range(4)]
            swapped = jnp.concatenate([parts[1], parts[0], parts[3], parts[2]], 0)
            return jnp.where(in_first_row, value, swapped)

        sums_0, sums_1 = by_lane(ordered(sums_ref), ordered(sums_other))
        z00, z11, z10 = sums_0[:NB], sums_1[:NB], sums_0[NB:] + sums_1[NB:]
        inv1_t, inv0_t = inv1.T, inv0.T
        cross = quick(inv1_t, z10)
        k1 = tril(a11 - quick(inv1_t, z11))
        e1 = diagonal_adjoint(tril(l1), k1, inv1_t, inv1)
        early = quick(a10 - cross, inv0)
        earlier = a00 - quick(inv0_t, z00 - quick(link.T, cross))
        g0 = early - quick(e1 + e1.T, quick(link, inv0))
        k0 = tril(earlier - quick(g0.T, link))
        e0 = diagonal_adjoint(tril(l0), k0, inv0_t, inv0)
        out_ref[...] = jnp.where(
            in_first_row, jnp.where(first, e0, 0.0), jnp.where(first, g0, e1)
        )


def place_kernel(n_pairs, ids, *refs):
    own, other, out_ref = refs[:n_pairs], refs[n_pairs:-1], refs[-1]
    first = ids[LANE] == 0
    for d in range(n_pairs):
        at = pl.ds(pl.multiple_of((ids[PAIR] ^ d) * NB, NB), NB)
        mine, theirs = own[d][...], other[d][...]
        out_ref[at, :NB] = jnp.where(first, mine, theirs)
        out_ref[at, NB:] = jnp.where(first, theirs, mine)


def after(value, *earlier):
    return lax.optimization_barrier((value, *earlier))[0]


def together(*values):
    return lax.optimization_barrier(values)


def local(factor, adjoint):
    n_rows = lax.axis_size("row")
    n_cols = lax.axis_size("col")
    n_pairs = n_cols // 2
    row_id = lax.axis_index("row")
    col_id = lax.axis_index("col")
    pair = col_id // 2
    lane = col_id % 2
    ids = jnp.stack([row_id, pair, lane])
    near = row_id // 2 == pair % 2
    first_pair = pair == 0
    local_rows = factor.shape[0]
    piece_rows = local_rows // 4

    def send(value, targets):
        edges = []
        for r in range(n_rows):
            for c in range(n_cols):
                target = targets(r, c // 2, c % 2)
                if target is not None:
                    edges.append((r * n_cols + c, target[0] * n_cols + target[1] * 2 + target[2]))
        return lax.ppermute(value, ("row", "col"), edges)

    def swap(value):
        return send(value, lambda r, p, k: (r, p, 1 - k))

    def swap_rows(value, d):
        return send(value, lambda r, p, k: (r ^ d, p, k))

    def swap_pairs(value, d):
        return send(value, lambda r, p, k: (r, p ^ d, k))

    panel = together(
        *[factor[i * piece_rows : (i + 1) * piece_rows, :NB] for i in range(4)], factor[:NB, :NB]
    )
    corner = panel[-1]

    def hop(value, number):
        return send(value, lambda r, p, k: (r, number, k) if p == number - 1 else None)

    def travel(value, hops):
        arrived = [value]
        for number in hops:
            arrived.append(hop(arrived[-1], number))
        return arrived

    def here(arrived):
        value = arrived[0]
        for p in range(1, len(arrived)):
            value = jnp.where(pair == p, arrived[p], value)
        return value

    middle = n_pairs // 2
    row_ids = jnp.arange(piece_rows, dtype=jnp.int32)
    trailing = ((row_ids >= NB) | (row_id >= 2))[:, None]

    def chosen(nearer, farther):
        start = pair // 2 % (piece_rows // NB) * NB
        value = here(nearer[:middle] + farther[middle:])
        return lax.dynamic_slice_in_dim(value, start, NB, 0)

    own_inverse = call(inverse_kernel, "inverse", SQUARE, ids, corner)
    carried = jnp.where((row_id == 1) & (lane == 0), corner, own_inverse)
    leading_piece = jnp.where(
        row_id < 2, jnp.concatenate([carried, panel[0][NB:]], 0), panel[0]
    )
    blocks = jnp.concatenate([corner, adjoint[:NB, :NB]], 0)
    across = send(blocks, lambda r, p, k: (r ^ 1, p, k) if p == 0 and r < 2 else None)
    every, nearest = range(1, n_pairs), range(1, middle)
    arrived_3, arrived_1, arrived_2 = [travel(panel[i], every) for i in (3, 1, 2)]
    arrived_0 = travel(leading_piece, nearest)
    carried = [x[:NB] for x in arrived_0]
    carried = carried + travel(carried[-1], range(middle, n_pairs - 1))[1:]
    high = swap_rows(chosen(arrived_2, arrived_3), 2)
    high, across, blocks, *rest = together(
        high, across, blocks, *arrived_3, *arrived_1, *arrived_2, *arrived_0, *carried
    )
    arrived_3, rest = rest[:n_pairs], rest[n_pairs:]
    arrived_1, rest = rest[:n_pairs], rest[n_pairs:]
    arrived_2, rest = rest[:n_pairs], rest[n_pairs:]
    arrived_0, carried = rest[:middle], rest[middle:]

    masked_0 = [jnp.where(trailing, x, 0.0) for x in arrived_0]
    low = chosen(masked_0, arrived_1)
    held = jnp.where(near, low, high)
    held = [held] + [swap_rows(held, d) for d in range(1, n_rows)]
    carried.append(hop(carried[-1], n_pairs - 1))
    columns = jax.ShapeDtypeStruct((local_rows, 2 * NB), jnp.bfloat16)
    half_columns = jax.ShapeDtypeStruct((local_rows // 2, 2 * NB), jnp.bfloat16)
    masked = call(
        functools.partial(mask_kernel, n_rows, n_cols),
        "masked",
        (columns, columns, half_columns, half_columns),
        ids,
        adjoint,
        swap(after(adjoint, high)),
    )
    pieces = here(masked_0), here(arrived_1), here(arrived_2), here(arrived_3)
    turned, low, *block_sums = call(
        functools.partial(column_kernel, n_rows),
        "columns",
        (
            jax.ShapeDtypeStruct((NB, local_rows), jnp.float32),
            jax.ShapeDtypeStruct((NB, 2 * NB), jnp.float32),
        )
        + (SQUARE,) * n_rows,
        ids,
        *masked,
        *pieces,
        scratch=(pltpu.VMEM((4, NB, NB), jnp.float32),),
    )

    across = jnp.where(first_pair, across, 0.0)
    across, *rest = together(across, *held, turned, low, *block_sums, *carried)
    held, (turned, low), rest = rest[:n_rows], rest[n_rows : n_rows + 2], rest[n_rows + 2 :]
    block_sums, carried = rest[:n_rows], rest[n_rows:]
    turned_other, blocks_other, across_other = swap(turned), swap(blocks), swap(across)

    height = 2 * NB // n_rows
    *evens, odds, product, carried = call(
        functools.partial(row_kernel, n_pairs),
        "rows",
        (SQUARE,) * middle
        + (
            jax.ShapeDtypeStruct((middle * NB, NB), jnp.float32),
            jax.ShapeDtypeStruct((local_rows, NB), jnp.float32),
            SQUARE,
        ),
        ids,
        *masked,
        *held,
        adjoint,
        *carried,
        scratch=(pltpu.VMEM((n_pairs, NB, NB), jnp.float32),),
    )
    slices = call(
        functools.partial(sum_kernel, n_rows),
        "sums",
        (jax.ShapeDtypeStruct((height, NB), jnp.float32),) * n_rows,
        ids,
        turned,
        turned_other,
        product,
        low,
        scratch=(pltpu.VMEM((n_rows, height, NB), jnp.float32),),
    )
    rest = together(blocks_other, across_other, carried, odds, *slices, *evens, *block_sums)
    (blocks_other, across_other, carried, odds), rest = rest[:4], rest[4:]
    slices, evens, block_sums = (
        rest[:n_rows],
        rest[n_rows : n_rows + middle],
        rest[n_rows + middle :],
    )

    def folded(values, bit):
        kept = {d: value for d, value in values.items() if not d & bit}
        moved = {d: swap_pairs(value, bit) for d, value in values.items() if d & bit}
        return kept, moved

    def added(kept, moved, bit):
        return {d: value + moved[d ^ bit] for d, value in kept.items()}

    slices = [slices[0]] + [swap_rows(slices[d], d) for d in range(1, n_rows)]
    beyond = send(carried, lambda r, p, k: (r + 2, p, k) if r < 2 else None)
    carried = jnp.where(row_id < 2, carried, beyond)
    rest = together(carried, swap_pairs(odds, 1), *block_sums, *slices, *evens)
    (carried, odds), rest = rest[:2], rest[2:]
    block_sums, rest = rest[:n_rows], rest[n_rows:]
    total, evens = sum(rest[1:n_rows], rest[0]), rest[n_rows:]
    own_share = evens[0]
    shares = {
        2 * i: evens[i] + odds[i * NB : (i + 1) * NB] for i in range(1, middle)
    }
    bit = 2
    while bit < n_pairs // 2:
        shares[0] = jnp.zeros_like(own_share)
        shares = added(*folded(shares, bit), bit)
        own_share = own_share + shares.pop(0)
        bit *= 2
    moved = swap_pairs(shares[bit], bit)
    def toward_first(value, bit):
        return send(
            value, lambda r, p, k: (r, p - bit, k) if p & bit and not p & (bit - 1) else None
        )

    bit = 1
    while bit < n_pairs // 2:
        total = total + toward_first(total, bit)
        bit *= 2
    total_other = toward_first(total, bit)
    block_sums = [block_sums[0]] + [swap_rows(block_sums[d], d) for d in range(1, n_rows)]
    rest = together(own_share, moved, odds, carried, total, total_other, *block_sums)
    own_share, moved, odds, carried, total, total_other = rest[:6]
    total, owned = total + total_other, sum(rest[7:], rest[6])

    def owner(r, p, k):
        half = 0 if r // 2 == p % 2 else 1
        return p % 2 * 2 + r % 2, p // 2 + half * (n_pairs // 2), k

    owned = send(owned, owner)
    carried = [carried, swap_rows(carried, 1)]
    sums = [total] + [
        send(total, lambda r, p, k, d=d: (r ^ d, p, k) if p == 0 and r ^ d < 2 else None)
        for d in range(1, n_rows)
    ]
    owned, *rest = together(owned, *carried, *sums)
    carried, sums = rest[:2], jnp.concatenate(rest[2:], 0)
    shares = own_share, moved, odds

    mine, solved = call(
        functools.partial(solve_kernel, 3), "solve", (SQUARE, SQUARE), ids, *shares, owned, *carried
    )
    second, sums_other = swap(solved), swap(sums)
    carried_other = [swap(x) for x in carried]
    result = call(
        end_kernel,
        "end",
        SQUARE,
        ids,
        mine,
        solved,
        second,
        *carried,
        *carried_other,
        blocks,
        across,
        blocks_other,
        across_other,
        sums,
        sums_other,
    )
    results, others, bit = {0: result}, {}, n_pairs // 2
    while bit:
        for d, value in list(results.items()):
            results[d ^ bit] = swap_pairs(value, bit)
        if bit == 2:
            results[1] = swap_pairs(result, 1)
            others[0] = swap(result)
            names = sorted(results)
            rest = together(others[0], *[results[d] for d in names])
            others[0], results = rest[0], dict(zip(names, rest[1:]))
            for d in names:
                if d ^ 1 not in results:
                    results[d ^ 1] = swap_pairs(results[d], 1)
            break
        bit //= 2
    for d in range(n_pairs):
        if d not in others:
            others[d] = swap(results[d])
    return call(
        functools.partial(place_kernel, n_pairs),
        "place",
        jax.ShapeDtypeStruct((local_rows, 2 * NB), jnp.float32),
        ids,
        *[results[d] for d in range(n_pairs)],
        *[others[d] for d in range(n_pairs)],
    )


def solution(mesh):
    placed = (P("row", "col"), P("row", "col"))
    return jax.shard_map(
        local, mesh=mesh, in_specs=placed, out_specs=P("row", None), check_vma=False
    )
```

```python
import functools

import jax
import jax.numpy as jnp
from jax import lax
from jax.experimental import pallas as pl
from jax.experimental.pallas import tpu as pltpu
from jax.sharding import PartitionSpec as P

NB = 256
ROW, PAIR, LANE = 0, 1, 2
SQUARE = jax.ShapeDtypeStruct((NB, NB), jnp.float32)


def dot(left, right):
    return jnp.dot(
        left, right, precision=lax.Precision.HIGHEST, preferred_element_type=jnp.float32
    )


def split(value):
    high = value.astype(jnp.bfloat16)
    return high, (value - high.astype(jnp.float32)).astype(jnp.bfloat16)


def dot3(left, right):
    once = functools.partial(jnp.dot, preferred_element_type=jnp.float32)
    return once(left[0], right[0]) + (once(left[0], right[1]) + once(left[1], right[0]))


def quick(left, right):
    return dot3(split(left), split(right))


def positions():
    rows = lax.broadcasted_iota(jnp.int32, (NB, NB), 0)
    cols = lax.broadcasted_iota(jnp.int32, (NB, NB), 1)
    return rows, cols


def call(kernel, name, out_shape, ids, *arrays, scratch=()):
    sizes = [x.size * x.dtype.itemsize for x in (*arrays, *jax.tree.leaves(out_shape))]
    return pl.pallas_call(
        kernel,
        out_shape=out_shape,
        in_specs=[pl.BlockSpec(memory_space=pltpu.SMEM)]
        + [pl.BlockSpec(memory_space=pltpu.VMEM)] * len(arrays),
        scratch_shapes=list(scratch),
        name=name,
        cost_estimate=pl.CostEstimate(flops=1, bytes_accessed=1, transcendentals=0),
        compiler_params=pltpu.CompilerParams(vmem_limit_bytes=min(60, 16 + sum(sizes) // 2**19) * 2**20),
    )(ids, *arrays)


def inverse_kernel(ids, block_ref, out_ref):
    @pl.when((ids[PAIR] == 0) & (ids[ROW] < 2))
    def _():
        half = NB // 2
        rows = lax.broadcasted_iota(jnp.int32, (half, half), 0)
        cols = lax.broadcasted_iota(jnp.int32, (half, half), 1)
        blocks = [block_ref[:half, :half], block_ref[half:, half:]]
        diagonal = rows == cols
        inverses = [
            jnp.where(diagonal, 1.0 / jnp.where(diagonal, x, 1.0), 0.0) for x in blocks
        ]
        size = 1
        while size < half:
            corner = (
                (rows // (2 * size) == cols // (2 * size))
                & (rows // size % 2 == 1)
                & (cols // size % 2 == 0)
            )
            inner = [dot(jnp.where(corner, x, 0.0), y) for x, y in zip(blocks, inverses)]
            inverses = [y - dot(y, x) for x, y in zip(inner, inverses)]
            size *= 2
        out_ref[:half, :half] = inverses[0]
        out_ref[:half, half:] = jnp.zeros((half, half), jnp.float32)
        out_ref[half:, half:] = inverses[1]
        out_ref[half:, :half] = -dot(inverses[1], dot(block_ref[half:, :half], inverses[0]))

    @pl.when((ids[PAIR] != 0) | (ids[ROW] >= 2))
    def _():
        out_ref[...] = jnp.zeros_like(out_ref)


def mask_kernel(n_rows, n_cols, ids, own, other, low_1, low_2, high_1, high_2):
    rows, cols = positions()
    below = rows - cols
    first = ids[LANE] == 0
    blocks = own.shape[0] // NB

    def masked(index, half, core):
        at = pl.ds(pl.multiple_of(index * NB, NB), NB)
        columns = slice(half * NB, (half + 1) * NB)
        mine = first if core == 0 else jnp.logical_not(first)
        value = jnp.where(mine, own[at, columns], other[at, columns])
        row_block = index * n_rows + ids[ROW]
        col_block = 2 * ids[PAIR] + half * n_cols + core
        least = jnp.where(row_block > col_block, -NB, jnp.where(row_block == col_block, 0, NB))
        least = jnp.where(row_block >= 2, least, NB)
        return split(jnp.where(below >= least, value, 0.0))

    @pl.loop(0, blocks)
    def _(index):
        for core in range(2):
            columns = slice(core * NB, (core + 1) * NB)
            at = pl.ds(pl.multiple_of(index * NB, NB), NB)
            low_1[at, columns], low_2[at, columns] = masked(index, 0, core)

    @pl.loop(0, blocks // 2)
    def _(index):
        for core in range(2):
            columns = slice(core * NB, (core + 1) * NB)
            at = pl.ds(pl.multiple_of(index * NB, NB), NB)
            high_1[at, columns], high_2[at, columns] = masked(index + blocks // 2, 1, core)


def column_kernel(n_rows, ids, low_1, low_2, high_1, high_2, *refs):
    refs, turned, low_ref, targets, sums = refs[:-7], refs[-7], refs[-6], refs[-5:-1], refs[-1]
    blocks = low_1.shape[0] // NB
    per_piece = blocks // 4
    low = jnp.zeros((NB, 2 * NB), jnp.float32)
    high = jnp.zeros((NB, 2 * NB), jnp.float32)
    for index, piece in enumerate(refs):
        for inner in range(per_piece):
            block = index * per_piece + inner
            at = slice(inner * NB, (inner + 1) * NB)
            value = piece[at, :]
            if block == 0:
                value = jnp.where(ids[ROW] >= 2, value, 0.0)
            value = value.T
            turned[:, block * NB : (block + 1) * NB] = value
            value = split(value)
            at = slice(block * NB, (block + 1) * NB)
            low += dot3(value, (low_1[at, :], low_2[at, :]))
            if block >= blocks // 2:
                block -= blocks // 2
                at = slice(block * NB, (block + 1) * NB)
                high += dot3(value, (high_1[at, :], high_2[at, :]))
    low_ref[...] = low
    sums[0], sums[1], sums[2], sums[3] = low[:, :NB], low[:, NB:], high[:, :NB], high[:, NB:]
    for d in range(n_rows):
        target = ids[ROW] ^ d
        targets[d][...] = sums[jnp.where(target // 2 == ids[PAIR] % 2, 0, 2) + target % 2]


def row_kernel(n_pairs, ids, low_1, low_2, high_1, high_2, v0, v1, v2, v3, adjoint, *refs):
    arrived, refs = refs[:n_pairs], refs[n_pairs:]
    evens, (odds, product_ref, carried, remaining) = refs[:-4], refs[-4:]
    pair, row = ids[PAIR], ids[ROW]
    x_is_0 = row % 2 == 0
    near = row // 2 == pair % 2

    def panel(same, across):
        return split(
            jnp.concatenate(
                [jnp.where(x_is_0, same, across), jnp.where(x_is_0, across, same)], 0
            )
        )

    v0, v1, v2, v3 = [ref[...] for ref in (v0, v1, v2, v3)]
    panel_low = panel(jnp.where(near, v0, v2), jnp.where(near, v1, v3))
    panel_high = panel(jnp.where(near, v2, v0), jnp.where(near, v3, v1))
    for block in range(n_pairs):
        at = slice(block * NB, (block + 1) * NB)
        product = dot3((low_1[at, :], low_2[at, :]), panel_low)
        if block >= n_pairs // 2:
            upper = slice((block - n_pairs // 2) * NB, (block - n_pairs // 2 + 1) * NB)
            product += dot3((high_1[upper, :], high_2[upper, :]), panel_high)
        remaining[block] = jnp.where(pair == 0, adjoint[at, :NB], 0.0) - product
        product_ref[at, :] = product
    for d in range(0, n_pairs, 2):
        evens[d // 2][...] = remaining[pair ^ d]
        odds[d // 2 * NB : (d // 2 + 1) * NB, :] = remaining[pair ^ (d + 1)]
    value = arrived[0][...]
    for p in range(1, n_pairs):
        value = jnp.where(pair == p, arrived[p][...], value)
    carried[...] = value


def sum_kernel(n_rows, ids, turned, turned_other, product_ref, low, *refs):
    slices, sums = refs[:-1], refs[-1]
    first, first_pair = ids[LANE] == 0, ids[PAIR] == 0
    own = jnp.zeros((NB, NB), jnp.float32)
    other = jnp.zeros((NB, NB), jnp.float32)
    for block in range(turned.shape[1] // NB):
        at = slice(block * NB, (block + 1) * NB)
        product = split(product_ref[at, :])
        own += dot3(split(turned[:, at]), product)
        other += dot3(split(turned_other[:, at]), product)
    own_term = jnp.where(first, low[:, :NB], low[:, NB:])
    own_term = jnp.where(first_pair, own_term, 0.0)
    cross_term = jnp.where(first_pair, low[:, NB:], 0.0)
    own_sum = (own_term - own).T - own
    other_sum = jnp.where(first, cross_term.T - other, -other.T)
    height = 2 * NB // n_rows
    for index in range(n_rows // 2):
        at = slice(index * height, (index + 1) * height)
        sums[index] = own_sum[at]
        sums[index + n_rows // 2] = other_sum[at]
    for d in range(n_rows):
        slices[d][...] = sums[ids[ROW] ^ d]


def carried_blocks(ids, refs):
    same, other = [ref[...] for ref in refs]
    even = ids[ROW] % 2 == 0
    link = jnp.where(even, other, same)
    return jnp.where(ids[LANE] == 0, jnp.where(even, same, other), link), link


def solve_kernel(n_pairs, ids, *refs):
    shares, owned, carried = refs[:n_pairs], refs[n_pairs], refs[n_pairs + 1 : -2]
    total_ref, solved = refs[-2:]
    total = shares[0][...]
    for ref in shares[1:]:
        total = total + ref[:NB, :]
    total = total - owned[...].T
    inverse, _ = carried_blocks(ids, carried)
    total_ref[...] = total
    solved[...] = quick(total, inverse)


def end_kernel(ids, total, solved, second, c0, c1, c0_other, c1_other, blocks, across, blocks_other, across_other, sums_ref, sums_other, out_ref):
    row, first = ids[ROW], ids[LANE] == 0
    own, other = (c0, c1), (c0_other, c1_other)
    leading = (ids[PAIR] == 0) & (row < 2)

    @pl.when(jnp.logical_not(leading))
    def _():
        inverse, link = carried_blocks(ids, own)
        whole = quick(total[...] - quick(second[...], link), inverse)
        out_ref[...] = jnp.where(first, whole, solved[...])

    @pl.when(leading)
    def _():
        rows, cols = positions()
        in_first_row = row == 0

        def tril(x):
            return jnp.where(rows >= cols, x, 0.0)

        def phi(x):
            return jnp.where(rows > cols, x, jnp.where(rows == cols, 0.5 * x, 0.0))

        def diagonal_adjoint(block, block_bar, inverse_t, inverse):
            inner = phi(quick(block.T, block_bar))
            s = quick(inverse_t, quick(inner, inverse))
            return phi(s + s.T)

        def by_lane(own, other):
            return jnp.where(first, own, other), jnp.where(first, other, own)

        def held(own, other):
            firsts, seconds = by_lane(own[...], other[...])
            return [x[i * NB : (i + 1) * NB] for x in (firsts, seconds) for i in range(2)]

        mine, theirs = held(blocks, blocks_other), held(across, across_other)
        l0, a00, _, _ = [jnp.where(in_first_row, a, b) for a, b in zip(mine, theirs)]
        link, a10, l1, a11 = [jnp.where(in_first_row, b, a) for a, b in zip(mine, theirs)]
        inv0, _ = by_lane(*[jnp.where(in_first_row, x[...], y[...]) for x, y in (own, other)])
        _, inv1 = by_lane(*[jnp.where(in_first_row, y[...], x[...]) for x, y in (own, other)])

        def ordered(ref):
            value = ref[...]
            height = value.shape[0] // 4
            parts = [value[i * height : (i + 1) * height] for i in range(4)]
            swapped = jnp.concatenate([parts[1], parts[0], parts[3], parts[2]], 0)
            return jnp.where(in_first_row, value, swapped)

        sums_0, sums_1 = by_lane(ordered(sums_ref), ordered(sums_other))
        z00, z11, z10 = sums_0[:NB], sums_1[:NB], sums_0[NB:] + sums_1[NB:]
        inv1_t, inv0_t = inv1.T, inv0.T
        cross = quick(inv1_t, z10)
        k1 = tril(a11 - quick(inv1_t, z11))
        e1 = diagonal_adjoint(tril(l1), k1, inv1_t, inv1)
        early = quick(a10 - cross, inv0)
        earlier = a00 - quick(inv0_t, z00 - quick(link.T, cross))
        g0 = early - quick(e1 + e1.T, quick(link, inv0))
        k0 = tril(earlier - quick(g0.T, link))
        e0 = diagonal_adjoint(tril(l0), k0, inv0_t, inv0)
        out_ref[...] = jnp.where(
            in_first_row, jnp.where(first, e0, 0.0), jnp.where(first, g0, e1)
        )


def place_kernel(n_pairs, ids, *refs):
    own, other, out_ref = refs[:n_pairs], refs[n_pairs:-1], refs[-1]
    first = ids[LANE] == 0
    for d in range(n_pairs):
        at = pl.ds(pl.multiple_of((ids[PAIR] ^ d) * NB, NB), NB)
        mine, theirs = own[d][...], other[d][...]
        out_ref[at, :NB] = jnp.where(first, mine, theirs)
        out_ref[at, NB:] = jnp.where(first, theirs, mine)


def after(value, *earlier):
    return lax.optimization_barrier((value, *earlier))[0]


def together(*values):
    return lax.optimization_barrier(values)


def local(factor, adjoint):
    n_rows = lax.axis_size("row")
    n_cols = lax.axis_size("col")
    n_pairs = n_cols // 2
    row_id = lax.axis_index("row")
    col_id = lax.axis_index("col")
    pair = col_id // 2
    lane = col_id % 2
    ids = jnp.stack([row_id, pair, lane])
    near = row_id // 2 == pair % 2
    first_pair = pair == 0
    local_rows = factor.shape[0]
    piece_rows = local_rows // 4

    def send(value, targets):
        edges = []
        for r in range(n_rows):
            for c in range(n_cols):
                target = targets(r, c // 2, c % 2)
                if target is not None:
                    edges.append((r * n_cols + c, target[0] * n_cols + target[1] * 2 + target[2]))
        return lax.ppermute(value, ("row", "col"), edges)

    def swap(value):
        return send(value, lambda r, p, k: (r, p, 1 - k))

    def swap_rows(value, d):
        return send(value, lambda r, p, k: (r ^ d, p, k))

    def swap_pairs(value, d):
        return send(value, lambda r, p, k: (r, p ^ d, k))

    panel = together(
        *[factor[i * piece_rows : (i + 1) * piece_rows, :NB] for i in range(4)], factor[:NB, :NB]
    )
    corner = panel[-1]

    def hop(value, number):
        return send(value, lambda r, p, k: (r, number, k) if p == number - 1 else None)

    def travel(value, hops):
        arrived = [value]
        for number in hops:
            arrived.append(hop(arrived[-1], number))
        return arrived

    def here(arrived):
        value = arrived[0]
        for p in range(1, len(arrived)):
            value = jnp.where(pair == p, arrived[p], value)
        return value

    middle = n_pairs // 2
    row_ids = jnp.arange(piece_rows, dtype=jnp.int32)
    trailing = ((row_ids >= NB) | (row_id >= 2))[:, None]

    def chosen(nearer, farther):
        start = pair // 2 % (piece_rows // NB) * NB
        value = here(nearer[:middle] + farther[middle:])
        return lax.dynamic_slice_in_dim(value, start, NB, 0)

    own_inverse = call(inverse_kernel, "inverse", SQUARE, ids, corner)
    carried = jnp.where((row_id == 1) & (lane == 0), corner, own_inverse)
    leading_piece = jnp.where(
        row_id < 2, jnp.concatenate([carried, panel[0][NB:]], 0), panel[0]
    )
    blocks = jnp.concatenate([corner, adjoint[:NB, :NB]], 0)
    across = send(blocks, lambda r, p, k: (r ^ 1, p, k) if p == 0 and r < 2 else None)
    every, nearest = range(1, n_pairs), range(1, middle)
    arrived_3, arrived_1, arrived_2 = [travel(panel[i], every) for i in (3, 1, 2)]
    arrived_0 = travel(leading_piece, nearest)
    carried = [x[:NB] for x in arrived_0]
    carried = carried + travel(carried[-1], range(middle, n_pairs - 1))[1:]
    high = swap_rows(chosen(arrived_2, arrived_3), 2)
    high, across, blocks, *rest = together(
        high, across, blocks, *arrived_3, *arrived_1, *arrived_2, *arrived_0, *carried
    )
    arrived_3, rest = rest[:n_pairs], rest[n_pairs:]
    arrived_1, rest = rest[:n_pairs], rest[n_pairs:]
    arrived_2, rest = rest[:n_pairs], rest[n_pairs:]
    arrived_0, carried = rest[:middle], rest[middle:]

    masked_0 = [jnp.where(trailing, x, 0.0) for x in arrived_0]
    low = chosen(masked_0, arrived_1)
    held = jnp.where(near, low, high)
    held = [held] + [swap_rows(held, d) for d in range(1, n_rows)]
    carried.append(hop(carried[-1], n_pairs - 1))
    columns = jax.ShapeDtypeStruct((local_rows, 2 * NB), jnp.bfloat16)
    half_columns = jax.ShapeDtypeStruct((local_rows // 2, 2 * NB), jnp.bfloat16)
    masked = call(
        functools.partial(mask_kernel, n_rows, n_cols),
        "masked",
        (columns, columns, half_columns, half_columns),
        ids,
        adjoint,
        swap(after(adjoint, high)),
    )
    pieces = here(masked_0), here(arrived_1), here(arrived_2), here(arrived_3)
    turned, low, *block_sums = call(
        functools.partial(column_kernel, n_rows),
        "columns",
        (
            jax.ShapeDtypeStruct((NB, local_rows), jnp.float32),
            jax.ShapeDtypeStruct((NB, 2 * NB), jnp.float32),
        )
        + (SQUARE,) * n_rows,
        ids,
        *masked,
        *pieces,
        scratch=(pltpu.VMEM((4, NB, NB), jnp.float32),),
    )

    across = jnp.where(first_pair, across, 0.0)
    across, *rest = together(across, *held, turned, low, *block_sums, *carried)
    held, (turned, low), rest = rest[:n_rows], rest[n_rows : n_rows + 2], rest[n_rows + 2 :]
    block_sums, carried = rest[:n_rows], rest[n_rows:]
    turned_other, blocks_other, across_other = swap(turned), swap(blocks), swap(across)

    height = 2 * NB // n_rows
    *evens, odds, product, carried = call(
        functools.partial(row_kernel, n_pairs),
        "rows",
        (SQUARE,) * middle
        + (
            jax.ShapeDtypeStruct((middle * NB, NB), jnp.float32),
            jax.ShapeDtypeStruct((local_rows, NB), jnp.float32),
            SQUARE,
        ),
        ids,
        *masked,
        *held,
        adjoint,
        *carried,
        scratch=(pltpu.VMEM((n_pairs, NB, NB), jnp.float32),),
    )
    slices = call(
        functools.partial(sum_kernel, n_rows),
        "sums",
        (jax.ShapeDtypeStruct((height, NB), jnp.float32),) * n_rows,
        ids,
        turned,
        turned_other,
        product,
        low,
        scratch=(pltpu.VMEM((n_rows, height, NB), jnp.float32),),
    )
    rest = together(blocks_other, across_other, carried, odds, *slices, *evens, *block_sums)
    (blocks_other, across_other, carried, odds), rest = rest[:4], rest[4:]
    slices, evens, block_sums = (
        rest[:n_rows],
        rest[n_rows : n_rows + middle],
        rest[n_rows + middle :],
    )

    def folded(values, bit):
        kept = {d: value for d, value in values.items() if not d & bit}
        moved = {d: swap_pairs(value, bit) for d, value in values.items() if d & bit}
        return kept, moved

    def added(kept, moved, bit):
        return {d: value + moved[d ^ bit] for d, value in kept.items()}

    slices = [slices[0]] + [swap_rows(slices[d], d) for d in range(1, n_rows)]
    beyond = send(carried, lambda r, p, k: (r + 2, p, k) if r < 2 else None)
    carried = jnp.where(row_id < 2, carried, beyond)
    rest = together(carried, swap_pairs(odds, 1), *block_sums, *slices, *evens)
    (carried, odds), rest = rest[:2], rest[2:]
    block_sums, rest = rest[:n_rows], rest[n_rows:]
    total, evens = sum(rest[1:n_rows], rest[0]), rest[n_rows:]
    own_share = evens[0]
    shares = {
        2 * i: evens[i] + odds[i * NB : (i + 1) * NB] for i in range(1, middle)
    }
    bit = 2
    while bit < n_pairs // 2:
        shares[0] = jnp.zeros_like(own_share)
        shares = added(*folded(shares, bit), bit)
        own_share = own_share + shares.pop(0)
        bit *= 2
    moved = swap_pairs(shares[bit], bit)
    def toward_first(value, bit):
        return send(
            value, lambda r, p, k: (r, p - bit, k) if p & bit and not p & (bit - 1) else None
        )

    bit = 1
    while bit < n_pairs // 2:
        total = total + toward_first(total, bit)
        bit *= 2
    total_other = toward_first(total, bit)
    block_sums = [block_sums[0]] + [swap_rows(block_sums[d], d) for d in range(1, n_rows)]
    rest = together(own_share, moved, odds, carried, total, total_other, *block_sums)
    own_share, moved, odds, carried, total, total_other = rest[:6]
    total, owned = total + total_other, sum(rest[7:], rest[6])

    def owner(r, p, k):
        half = 0 if r // 2 == p % 2 else 1
        return p % 2 * 2 + r % 2, p // 2 + half * (n_pairs // 2), k

    owned = send(owned, owner)
    carried = [carried, swap_rows(carried, 1)]
    sums = [total] + [
        send(total, lambda r, p, k, d=d: (r ^ d, p, k) if p == 0 and r ^ d < 2 else None)
        for d in range(1, n_rows)
    ]
    owned, *rest = together(owned, *carried, *sums)
    carried, sums = rest[:2], jnp.concatenate(rest[2:], 0)
    shares = own_share, moved, odds

    mine, solved = call(
        functools.partial(solve_kernel, 3), "solve", (SQUARE, SQUARE), ids, *shares, owned, *carried
    )
    second, sums_other = swap(solved), swap(sums)
    carried_other = [swap(x) for x in carried]
    result = call(
        end_kernel,
        "end",
        SQUARE,
        ids,
        mine,
        solved,
        second,
        *carried,
        *carried_other,
        blocks,
        across,
        blocks_other,
        across_other,
        sums,
        sums_other,
    )
    results, others, bit = {0: result}, {}, n_pairs // 2
    while bit:
        for d, value in list(results.items()):
            results[d ^ bit] = swap_pairs(value, bit)
        if bit == 2:
            results[1] = swap_pairs(result, 1)
            others[0] = swap(result)
            names = sorted(d for d in results if d != 1)
            nearest = results[1]
            rest = together(others[0], *[results[d] for d in names])
            others[0], results = rest[0], dict(zip(names, rest[1:]))
            results[1] = nearest
            for d in names:
                if d ^ 1 not in results:
                    results[d ^ 1] = swap_pairs(results[d], 1)
            break
        bit //= 2
    for d in range(n_pairs):
        if d not in others:
            others[d] = swap(results[d])
    return call(
        functools.partial(place_kernel, n_pairs),
        "place",
        jax.ShapeDtypeStruct((local_rows, 2 * NB), jnp.float32),
        ids,
        *[results[d] for d in range(n_pairs)],
        *[others[d] for d in range(n_pairs)],
    )


def solution(mesh):
    placed = (P("row", "col"), P("row", "col"))
    return jax.shard_map(
        local, mesh=mesh, in_specs=placed, out_specs=P("row", None), check_vma=False
    )
```
